128 devices in a mesh: dp: 8 (over y_lo, x), axial: 16 (over z, y_hi, core).
Axes of the slice: x: 4, y: 4 (y_hi: 2, y_lo: 2; y = y_hi * 2 + y_lo), z: 4, core: 2. Of those that a mesh axis runs over, the one named last changes fastest.
Arguments:
- pair: bfloat16 [8, 256, 256, 128], P('dp', 'axial'), may hold values from -6 to 6
- cotangent: bfloat16 [8, 256, 256, 128], P('dp', 'axial'), may hold values from -6 to 6
- in_weight: bfloat16 [128, 640], replicated, may hold values from -0.5 to 0.5
- out_weight: bfloat16 [128, 128], replicated, may hold values from -0.5 to 0.5
- gain_in: float32 [128], replicated, may hold values from 0.5 to 1.5
- gain_x: float32 [128], replicated, may hold values from 0.5 to 1.5
Outputs:
- updated: bfloat16 [8, 256, 256, 128], P('dp', 'axial')
- grad_pair: bfloat16 [8, 256, 256, 128], P('dp', 'axial')
- grad_in_weight: float32 [128, 640], replicated
- grad_out_weight: float32 [128, 128], replicated
- grad_gain_in: float32 [128], replicated
- grad_gain_x: float32 [128], replicated
The draws below stay inside these ranges and needn't reach their ends.
All inputs are finite; a program needn't handle non-finite values.
Results may differ from the reference program's by a relative error of at most 0.015.
Values may be sent and summed in bfloat16 or wider, within the bound.
A program may use at most 192 MiB of HBM per device.

```python
import jax
import jax.numpy as jnp
from jax import lax

PAIR = 128
HIDDEN_SIZE = 128
CROP = 256
CROPS = 8
N_AXIAL = 16


def strengthened(entries, stream_key, source, target, blocks, factor):
    def block_of(dim):
        return (jnp.arange(entries.shape[dim]) // (entries.shape[dim] // blocks)).reshape((-1,) + (1,) * (entries.ndim - 1 - dim))

    first = jax.random.permutation(stream_key, blocks)[block_of(target)]
    far = (block_of(target) + blocks // 2) % blocks
    return jnp.where((block_of(source) == first) | (block_of(source) == far), factor * entries, entries)


def level_of(key, extent, cuts, low, high):
    def one(position, blocks):
        steps = jax.random.uniform(jax.random.fold_in(jax.random.fold_in(key, 6), position), (blocks,), jnp.float32, low / len(cuts), high / len(cuts))
        return jnp.repeat(jnp.exp(steps), extent[position] // blocks).reshape((-1,) + (1,) * (len(extent) - position - 1))

    level = one(*cuts[0])
    for cut in cuts[1:]:
        level = level * one(*cut)
    return level


def centred(rng, dims, deviation, limit, shards=(), kind=jnp.bfloat16):
    factor_of = level_of(rng, dims, shards, -0.22, 0.18) if shards else 1.0
    entries = jax.random.normal(rng, dims, jnp.float32) * deviation * factor_of
    return jnp.minimum(jnp.maximum(entries, -limit), limit).astype(kind)


def bell_draw_with(stream_key, extent, width, reach, pieces, heavy, kind=jnp.bfloat16):
    drawn = width * jax.random.normal(stream_key, extent, jnp.float32)
    if pieces:
        drawn = drawn * level_of(stream_key, extent, pieces, -0.22, 0.18)
    return jnp.clip(strengthened(drawn, jax.random.fold_in(stream_key, 3), *heavy), -reach, reach).astype(kind)


def setup_inputs(seed: int = 0) -> dict:
    splits = jax.random.split(jax.random.key(seed), 7)
    pair = centred(splits[0], (CROPS, CROP, CROP, PAIR), 1.0, 6.0, ((0, 8), (1, 16)))
    cotangent = bell_draw_with(splits[1], (CROPS, CROP, CROP, PAIR), 1.0, 6.0, ((0, 8), (1, 16)), (1, 2, 16, 2.0))
    in_weight = centred(splits[2], (PAIR, 4 * HIDDEN_SIZE + PAIR), PAIR ** -0.5, 0.5)
    out_weight = centred(splits[3], (HIDDEN_SIZE, PAIR), HIDDEN_SIZE ** -0.5, 0.5)
    gain_in = jnp.clip(jax.random.uniform(splits[4], (PAIR,), jnp.float32, 0.5, 1.5), 0.5, 1.5)
    gain_x = jnp.clip(jax.random.uniform(splits[5], (HIDDEN_SIZE,), jnp.float32, 0.5, 1.5), 0.5, 1.5)
    return dict(pair=pair, cotangent=cotangent, in_weight=in_weight, out_weight=out_weight, gain_in=gain_in, gain_x=gain_x)


def norm_stats(values, gain):
    center = lax.optimization_barrier(jnp.mean(values, axis=-1, keepdims=True))
    shifted = values - center
    spread = jnp.sqrt(lax.optimization_barrier(jnp.mean(shifted * shifted, axis=-1, keepdims=True)) + 1e-05)
    unit_val = shifted / spread
    return (unit_val * gain, unit_val, spread)

def norm_back(grad_norm, unit_val, spread, gain):
    scaled = grad_norm * gain
    mean_one = lax.optimization_barrier(jnp.mean(scaled, axis=-1, keepdims=True))
    mean_two = lax.optimization_barrier(jnp.mean(scaled * unit_val, axis=-1, keepdims=True))
    return (scaled - mean_one - unit_val * mean_two) / spread

def one_crop(pair_crop, upstream, in_weight, out_weight, gain_in, gain_x):
    normed, unit_in, spread_in = norm_stats(pair_crop.astype(jnp.float32), gain_in)
    normed = normed.astype(jnp.bfloat16)
    flat_in = normed.reshape(CROP * CROP, PAIR)
    projected = jnp.dot(flat_in, in_weight, preferred_element_type=jnp.float32).reshape(CROP, CROP, 4 * HIDDEN_SIZE + PAIR)
    proj_a = projected[..., :HIDDEN_SIZE]
    gate_a = jax.nn.sigmoid(projected[..., HIDDEN_SIZE:2 * HIDDEN_SIZE])
    proj_b = projected[..., 2 * HIDDEN_SIZE:3 * HIDDEN_SIZE]
    gate_b = jax.nn.sigmoid(projected[..., 3 * HIDDEN_SIZE:4 * HIDDEN_SIZE])
    gate_out = jax.nn.sigmoid(projected[..., 4 * HIDDEN_SIZE:])
    left = (gate_a * proj_a).astype(jnp.bfloat16)
    right = (gate_b * proj_b).astype(jnp.bfloat16)
    left_f = left.astype(jnp.float32)
    right_f = right.astype(jnp.float32)
    product = jnp.einsum('ikc,jkc->ijc', left_f, right_f)
    xnorm, unit_x, spread_x = norm_stats(product, gain_x)
    xnorm = xnorm.astype(jnp.bfloat16)
    flat_x = xnorm.reshape(CROP * CROP, HIDDEN_SIZE)
    lifted = jnp.dot(flat_x, out_weight, preferred_element_type=jnp.float32).reshape(CROP, CROP, PAIR)
    updated = (gate_out * lifted).astype(jnp.bfloat16)
    upstream_f = upstream.astype(jnp.float32)
    grad_lift = (upstream_f * gate_out).astype(jnp.bfloat16)
    grad_gate = upstream_f * lifted * gate_out * (1.0 - gate_out)
    flat_lift = grad_lift.reshape(CROP * CROP, PAIR)
    local_out = jnp.dot(flat_x.T, flat_lift, preferred_element_type=jnp.float32)
    grad_xnorm = jnp.dot(flat_lift, out_weight.T, preferred_element_type=jnp.float32).reshape(CROP, CROP, HIDDEN_SIZE)
    local_gx = lax.optimization_barrier(jnp.sum(grad_xnorm * unit_x, axis=(0, 1)))
    grad_prod = norm_back(grad_xnorm, unit_x, spread_x, gain_x).astype(jnp.bfloat16)
    grad_prod_f = grad_prod.astype(jnp.float32)
    grad_left = jnp.einsum('ijc,jkc->ikc', grad_prod_f, right_f)
    block = CROP // N_AXIAL

    def add_block(total, index):
        start = (index * block).astype(jnp.int32)
        sub_grad = lax.dynamic_slice_in_dim(grad_prod_f, start, block, 0)
        sub_left = lax.dynamic_slice_in_dim(left_f, start, block, 0)
        partial_sum = jnp.einsum('ijc,ikc->jkc', sub_grad, sub_left).astype(jnp.bfloat16)
        partial_sum = lax.optimization_barrier(partial_sum)
        return (total + partial_sum.astype(jnp.float32), None)
    grad_right, _ = lax.scan(add_block, jnp.zeros((CROP, CROP, HIDDEN_SIZE), jnp.float32), jnp.arange(N_AXIAL, dtype=jnp.int32))
    grad_proj = jnp.concatenate([grad_left * gate_a, grad_left * proj_a * gate_a * (1.0 - gate_a), grad_right * gate_b, grad_right * proj_b * gate_b * (1.0 - gate_b), grad_gate], axis=-1).astype(jnp.bfloat16)
    flat_proj = grad_proj.reshape(CROP * CROP, 4 * HIDDEN_SIZE + PAIR)
    local_in = jnp.dot(flat_in.T, flat_proj, preferred_element_type=jnp.float32)
    grad_normed = jnp.dot(flat_proj, in_weight.T, preferred_element_type=jnp.float32).reshape(CROP, CROP, PAIR)
    local_gi = lax.optimization_barrier(jnp.sum(grad_normed * unit_in, axis=(0, 1)))
    grad_pair = norm_back(grad_normed, unit_in, spread_in, gain_in).astype(jnp.bfloat16)
    return (updated, grad_pair, local_in, local_out, local_gi, local_gx)

def reference(pair, cotangent, in_weight, out_weight, gain_in, gain_x):

    def step(totals, crop_args):
        updated, grad_pair, local_in, local_out, local_gi, local_gx = one_crop(crop_args[0], crop_args[1], in_weight, out_weight, gain_in, gain_x)
        totals = (totals[0] + local_in, totals[1] + local_out, totals[2] + local_gi, totals[3] + local_gx)
        return (totals, (updated, grad_pair))
    start_tot = (jnp.zeros((PAIR, 4 * HIDDEN_SIZE + PAIR), jnp.float32), jnp.zeros((HIDDEN_SIZE, PAIR), jnp.float32), jnp.zeros((PAIR,), jnp.float32), jnp.zeros((HIDDEN_SIZE,), jnp.float32))
    totals, stacked = lax.scan(step, start_tot, (pair, cotangent))
    factor = 1.0 / jnp.sqrt(jnp.float32(CROPS * CROP * CROP))
    return (stacked[0], stacked[1], totals[0] * factor, totals[1] * factor, totals[2] * factor, totals[3] * factor)
```

```python
import functools

import jax
import jax.numpy as jnp
from jax import lax
from jax.experimental import pallas as pl
from jax.experimental.pallas import tpu as pltpu
from jax.sharding import PartitionSpec as P

MESH = pl.DeviceIdType.MESH
F32 = jnp.float32
BF16 = jnp.bfloat16
LEFT, RIGHT, PROD, GPROD, GLEFT, GRIGHT = range(6)


def dot(a, b):
    return lax.dot_general(a, b, (((1,), (0,)), ((), ())), preferred_element_type=F32)


def dot_nt(a, b):
    return lax.dot_general(a, b, (((1,), (1,)), ((), ())), preferred_element_type=F32)


def dot_tn(a, b):
    return lax.dot_general(a, b, (((0,), (0,)), ((), ())), preferred_element_type=F32)


def sigmoid(v):
    return 0.5 * jnp.tanh(0.5 * v) + 0.5


def stats(v):
    center = jnp.mean(v, axis=0, keepdims=True)
    shifted = v - center
    inv = lax.rsqrt(jnp.mean(shifted * shifted, axis=0, keepdims=True) + 1e-05)
    return shifted * inv, inv


def kernel(
    n_dp, n_ax, factor,
    pair, cot, w_in, w_out, gain_in, gain_x,
    upd, gpair, gw_in, gw_out, ggi, ggx,
    send, recv, tbuf, tbuf2, lc, rc, gc,
    normed, unit_in, inv_in, gate_a, q_a, gate_b, q_b, gate_o, s_x, c_g, glift, xnorm, gnorm,
    w_t, wo_t, gin, gx, dw, r1, r2, s1, s2, fin,
    ssem, rsem, lsem, asend, arecv,
):
    me = lax.axis_index("axial")
    dp = lax.axis_index("dp")
    my_z, my_y, my_c = me // 4, (me // 2) % 2, me % 2

    def peer(o):
        return ((my_z + o // 4) % 4) * 4 + ((my_y + (o // 2) % 2) % 2) * 2 + (my_c + o % 2) % 2

    def dp_peer(o):
        return (dp + o) % n_dp

    def each(lo, hi, fn, unroll=1):
        def body(i, carry):
            fn(i)
            return carry
        lax.fori_loop(lo, hi, body, 0, unroll=unroll)

    barrier = pltpu.get_barrier_semaphore()
    each(1, n_ax, lambda o: pl.semaphore_signal(
        barrier, inc=1, device_id=(dp, peer(o)), device_id_type=MESH))
    each(1, n_dp, lambda o: pl.semaphore_signal(
        barrier, inc=1, device_id=(dp_peer(o), me), device_id_type=MESH))

    def start(t):
        def one(o):
            d = peer(o)
            pltpu.make_async_remote_copy(
                src_ref=send.at[t, d], dst_ref=recv.at[t, me],
                send_sem=ssem.at[t], recv_sem=rsem.at[t],
                device_id=(dp, d), device_id_type=MESH).start()
        each(1, n_ax, one)
        pltpu.make_async_copy(send.at[t, me], recv.at[t, me], lsem.at[t]).start()

    def wait_recv(t):
        pltpu.make_async_copy(send.at[t, me], recv.at[t, me], lsem.at[t]).wait()
        part = recv.at[t, pl.ds(0, n_ax - 1)]
        pltpu.make_async_copy(part, part, rsem.at[t]).wait()

    def wait_send(t):
        part = send.at[t, pl.ds(0, n_ax - 1)]
        pltpu.make_async_copy(part, part, ssem.at[t]).wait()

    def reduce_start(p):
        def one(o):
            d = peer(o)
            pltpu.make_async_remote_copy(
                src_ref=dw.at[p, pl.ds(8 * d, 8)], dst_ref=r1.at[p, me],
                send_sem=asend.at[p], recv_sem=arecv.at[p],
                device_id=(dp, d), device_id_type=MESH).start()
        each(1, n_ax, one)
        r1[p, me] = dw[p, pl.ds(8 * me, 8)]

    def reduce_dp(p):
        part = r1.at[p, pl.ds(0, n_ax - 1)]
        pltpu.make_async_copy(part, part, arecv.at[p]).wait()
        total = jnp.sum(r1[p], axis=0)
        s1[p] = total
        r2[p, dp] = total

        def one(o):
            pltpu.make_async_remote_copy(
                src_ref=s1.at[p], dst_ref=r2.at[p, dp],
                send_sem=asend.at[3 + p], recv_sem=arecv.at[3 + p],
                device_id=(dp_peer(o), me), device_id_type=MESH).start()
        each(1, n_dp, one)

    def reduce_back(p):
        part = r2.at[p, pl.ds(0, n_dp - 1)]
        pltpu.make_async_copy(part, part, arecv.at[3 + p]).wait()
        total = jnp.sum(r2[p], axis=0) * factor
        s2[p] = total
        fin[p, me] = total

        def one(o):
            pltpu.make_async_remote_copy(
                src_ref=s2.at[p], dst_ref=fin.at[p, me],
                send_sem=asend.at[6 + p], recv_sem=arecv.at[6 + p],
                device_id=(dp, peer(o)), device_id_type=MESH).start()
        each(1, n_ax, one)

    def reduce_end(p):
        part = fin.at[p, pl.ds(0, n_ax - 1)]
        pltpu.make_async_copy(part, part, arecv.at[6 + p]).wait()

    def reduce_sent(p):
        part = r1.at[p, pl.ds(0, n_ax - 1)]
        pltpu.make_async_copy(part, part, asend.at[p]).wait()
        part = r2.at[p, pl.ds(0, n_dp - 1)]
        pltpu.make_async_copy(part, part, asend.at[3 + p]).wait()
        part = fin.at[p, pl.ds(0, n_ax - 1)]
        pltpu.make_async_copy(part, part, asend.at[6 + p]).wait()

    def strided(i):
        return pl.ds(i, 128, stride=8)

    def put(k, values):
        tbuf2[0, strided(k), :] = values[:, :128]
        tbuf2[1, strided(k), :] = values[:, 128:]

    def take(k):
        return jnp.concatenate([tbuf[0, strided(k), :], tbuf[1, strided(k), :]], axis=1)

    def flush(t):
        for n in range(2):
            send[t, :, :, 128 * n:128 * (n + 1)] = tbuf2[n].astype(BF16).reshape(16, 64, 128)

    def unpack(t):
        for n in range(2):
            tbuf[n] = recv[t, :, :, 128 * n:128 * (n + 1)].astype(F32).reshape(1024, 128)

    def load_pair(t, cp):
        both = recv[t, :, pl.ds(pl.multiple_of(16 * cp, 16), 16), :].astype(F32).reshape(16, 2, 8, 256)
        return both[:, 0], both[:, 1]

    def store_pair(t, cp, even, odd):
        both = jnp.concatenate([even, odd], axis=1).astype(BF16)
        send[t, :, pl.ds(pl.multiple_of(16 * cp, 16), 16), :] = both

    w_t[...] = w_in[...].astype(F32).T.astype(BF16)
    wo_t[...] = w_out[...].astype(F32).T.astype(BF16)
    gin[...] = jnp.broadcast_to(jnp.broadcast_to(gain_in[...], (128, 128)).T[:, :1], (128, 256))
    gx[...] = jnp.broadcast_to(jnp.broadcast_to(gain_x[...], (128, 128)).T[:, :1], (128, 256))

    for h in range(2):
        def left_row(k):
            i = 8 * h + k
            unit, inv = stats(pair[i].astype(F32).T)
            unit_in[i] = unit
            inv_in[i] = inv
            flat = (unit * gin[...]).astype(BF16)
            normed[i] = flat
            projected = dot(w_t[0:256], flat)
            value, gate = projected[:128], sigmoid(projected[128:])
            left = value * gate
            gate_a[i] = gate
            q_a[i] = left * (1.0 - gate)
            put(k, left)
        each(0, 8, left_row)
        flush(2 * LEFT + h)
        if h == 0:
            pl.semaphore_wait(barrier, n_ax - 1 + n_dp - 1)
        start(2 * LEFT + h)

    for h in range(2):
        def right_row(k):
            i = 8 * h + k
            projected = dot(w_t[256:512], normed[i])
            value, gate = projected[:128], sigmoid(projected[128:])
            right = value * gate
            gate_b[i] = gate
            q_b[i] = right * (1.0 - gate)
            put(k, right)
        each(0, 8, right_row)
        flush(2 * RIGHT + h)
        start(2 * RIGHT + h)

    def gate_row(i):
        gate = sigmoid(dot(w_t[512:640], normed[i]))
        upstream = cot[i].astype(F32).T
        lift = upstream * gate
        gate_o[i] = gate
        c_g[i] = lift * (1.0 - gate)
        lift = lift.astype(BF16)
        glift[i] = lift
        s_x[i] = dot(w_out[...], lift) * gx[...]
    each(0, 16, gate_row)

    for t in (2 * LEFT, 2 * LEFT + 1, 2 * RIGHT, 2 * RIGHT + 1):
        wait_recv(t)

    def product_pair(cp):
        left0, left1 = load_pair(2 * LEFT, cp), load_pair(2 * LEFT + 1, cp)
        right0, right1 = load_pair(2 * RIGHT, cp), load_pair(2 * RIGHT + 1, cp)
        prods = []
        for e in range(2):
            left = jnp.concatenate([left0[e], left1[e]], axis=0).reshape(256, 256).astype(BF16)
            right = jnp.concatenate([right0[e], right1[e]], axis=1).reshape(256, 256).astype(BF16)
            lc[2 * cp + e] = left
            rc[2 * cp + e] = right
            prods.append(dot_nt(left, right).reshape(2, 16, 8, 256))
        for h in range(2):
            store_pair(2 * PROD + h, cp, prods[0][h], prods[1][h])
    each(0, 4, product_pair)
    start(2 * PROD)
    start(2 * PROD + 1)

    for h in range(2):
        wait_recv(2 * PROD + h)
        unpack(2 * PROD + h)

        def norm_row(k):
            i = 8 * h + k
            unit, inv = stats(take(k))
            xnorm[i] = (unit * gx[...]).astype(BF16)
            scaled = s_x[i]
            mean_one = jnp.mean(scaled, axis=0, keepdims=True)
            mean_two = jnp.mean(scaled * unit, axis=0, keepdims=True)
            put(k, (scaled - mean_one - unit * mean_two) * inv)
        each(0, 8, norm_row)
        flush(2 * GPROD + h)
        start(2 * GPROD + h)

    dw[...] = jnp.zeros_like(dw)

    def lift_row(i):
        flat = xnorm[i]
        lifted = dot(wo_t[...], flat)
        upd[i] = (gate_o[i] * lifted).T.astype(BF16)
        ggate = (lifted * c_g[i]).astype(BF16)
        dw[0, :, 0:128] += dot_nt(flat, glift[i])
        dw[0, :, 128:256] += dot_nt(normed[i], ggate)
        gnorm[i] = dot(w_in[:, 512:640], ggate)
    each(0, 16, lift_row)
    reduce_start(0)

    for h in range(2):
        wait_recv(2 * GPROD + h)

        def gleft_pair(cp):
            grads = load_pair(2 * GPROD + h, cp)
            outs = []
            for e in range(2):
                grad = grads[e].reshape(128, 256).astype(BF16)
                gc[2 * cp + e, pl.ds(128 * h, 128), :] = grad
                outs.append(dot(grad, rc[2 * cp + e]).reshape(16, 8, 256))
            store_pair(2 * GLEFT + h, cp, outs[0], outs[1])
        each(0, 4, gleft_pair)
        start(2 * GLEFT + h)

    def gright_pair(cp):
        outs = [dot_tn(gc[2 * cp + e], lc[2 * cp + e]).reshape(16, 2, 8, 256) for e in range(2)]
        for h in range(2):
            store_pair(2 * GRIGHT + h, cp, outs[0][:, h], outs[1][:, h])
    each(0, 4, gright_pair)
    start(2 * GRIGHT)
    start(2 * GRIGHT + 1)
    reduce_dp(0)

    def back(a, p, lo, gate_ref, q_ref):
        for h in range(2):
            wait_recv(2 * a + h)
            unpack(2 * a + h)

            def back_row(k):
                i = 8 * h + k
                grad = take(k)
                both = jnp.concatenate([grad * gate_ref[i], grad * q_ref[i]], axis=0).astype(BF16)
                dw[p] += dot_nt(normed[i], both)
                gnorm[i] += dot(w_in[:, lo:lo + 256], both)
            each(0, 8, back_row)

    back(GLEFT, 1, 0, gate_a, q_a)
    reduce_start(1)
    reduce_back(0)
    reduce_dp(1)
    back(GRIGHT, 2, 256, gate_b, q_b)
    reduce_start(2)
    reduce_back(1)

    def out_row(i):
        unit = unit_in[i]
        scaled = gnorm[i] * gin[...]
        mean_one = jnp.mean(scaled, axis=0, keepdims=True)
        mean_two = jnp.mean(scaled * unit, axis=0, keepdims=True)
        gpair[i] = ((scaled - mean_one - unit * mean_two) * inv_in[i]).T.astype(BF16)
    each(0, 8, out_row)
    reduce_dp(2)
    each(8, 16, out_row)
    reduce_back(2)
    reduce_end(0)
    reduce_end(1)
    reduce_end(2)

    first = fin[0].reshape(128, 256)
    gw_out[...] = first[:, :128]
    gw_in[:, 512:640] = first[:, 128:]
    gw_in[:, 0:256] = fin[1].reshape(128, 256)
    gw_in[:, 256:512] = fin[2].reshape(128, 256)
    row_in = jnp.sum(gw_in[...] * w_in[...].astype(F32), axis=1, keepdims=True)
    row_x = jnp.sum(gw_out[...] * w_out[...].astype(F32), axis=1, keepdims=True)
    ggi[...] = jnp.broadcast_to(row_in, (128, 128)).T[:1] / gain_in[...]
    ggx[...] = jnp.broadcast_to(row_x, (128, 128)).T[:1] / gain_x[...]

    for t in range(12):
        wait_send(t)
    for p in range(3):
        reduce_sent(p)


def local(n_dp, n_ax, pair, cotangent, in_weight, out_weight, gain_in, gain_x):
    rows, width, chan = pair.shape[1:]
    factor = 1.0 / (n_dp * width * width) ** 0.5
    vmem = pl.BlockSpec(memory_space=pltpu.VMEM)
    cells = (rows, chan, width)
    outs = pl.pallas_call(
        functools.partial(kernel, n_dp, n_ax, factor),
        name="triangle",
        out_shape=(
            jax.ShapeDtypeStruct((rows, width, chan), BF16),
            jax.ShapeDtypeStruct((rows, width, chan), BF16),
            jax.ShapeDtypeStruct((128, 640), F32),
            jax.ShapeDtypeStruct((128, 128), F32),
            jax.ShapeDtypeStruct((1, 128), F32),
            jax.ShapeDtypeStruct((1, 128), F32),
        ),
        in_specs=[vmem] * 6,
        out_specs=(vmem,) * 6,
        scratch_shapes=[
            pltpu.VMEM((12, 16, 64, 256), BF16),
            pltpu.VMEM((12, 16, 64, 256), BF16),
            pltpu.VMEM((2, 1024, 128), F32),
            pltpu.VMEM((2, 1024, 128), F32),
            pltpu.VMEM((8, 256, 256), BF16),
            pltpu.VMEM((8, 256, 256), BF16),
            pltpu.VMEM((8, 256, 256), BF16),
            pltpu.VMEM(cells, BF16),
            pltpu.VMEM(cells, F32),
            pltpu.VMEM((rows, 1, width), F32),
            pltpu.VMEM(cells, F32),
            pltpu.VMEM(cells, F32),
            pltpu.VMEM(cells, F32),
            pltpu.VMEM(cells, F32),
            pltpu.VMEM(cells, F32),
            pltpu.VMEM(cells, F32),
            pltpu.VMEM(cells, F32),
            pltpu.VMEM(cells, BF16),
            pltpu.VMEM(cells, BF16),
            pltpu.VMEM(cells, F32),
            pltpu.VMEM((640, 128), BF16),
            pltpu.VMEM((128, 128), BF16),
            pltpu.VMEM((128, 256), F32),
            pltpu.VMEM((128, 256), F32),
            pltpu.VMEM((3, 128, 256), F32),
            pltpu.VMEM((3, 16, 8, 256), F32),
            pltpu.VMEM((3, 8, 8, 256), F32),
            pltpu.VMEM((3, 8, 256), F32),
            pltpu.VMEM((3, 8, 256), F32),
            pltpu.VMEM((3, 16, 8, 256), F32),
            pltpu.SemaphoreType.DMA((12,)),
            pltpu.SemaphoreType.DMA((12,)),
            pltpu.SemaphoreType.DMA((12,)),
            pltpu.SemaphoreType.DMA((9,)),
            pltpu.SemaphoreType.DMA((9,)),
        ],
        compiler_params=pltpu.CompilerParams(
            collective_id=0, has_side_effects=True, vmem_limit_bytes=60 * 2**20),
        cost_estimate=pl.CostEstimate(
            flops=3_300_000_000, bytes_accessed=5_000_000, transcendentals=1_600_000),
    )(pair[0], cotangent[0], in_weight, out_weight, gain_in[None], gain_x[None])
    upd, gpair, gw_in, gw_out, ggi, ggx = outs
    return upd[None], gpair[None], gw_in, gw_out, ggi[0], ggx[0]


def solution(mesh):
    cells = P("dp", "axial", None, None)
    n_dp, n_ax = mesh.shape["dp"], mesh.shape["axial"]
    return jax.shard_map(
        functools.partial(local, n_dp, n_ax), mesh=mesh,
        in_specs=(cells, cells, P(), P(), P(), P()),
        out_specs=(cells, cells, P(), P(), P(), P()), check_vma=False)
```

```python
import functools

import jax
import jax.numpy as jnp
from jax import lax
from jax.experimental import pallas as pl
from jax.experimental.pallas import tpu as pltpu
from jax.sharding import PartitionSpec as P

MESH = pl.DeviceIdType.MESH
F32 = jnp.float32
BF16 = jnp.bfloat16
LEFT, RIGHT, PROD, GPROD, GLEFT, GRIGHT = range(6)


def dot(a, b):
    return lax.dot_general(a, b, (((1,), (0,)), ((), ())), preferred_element_type=F32)


def dot_nt(a, b):
    return lax.dot_general(a, b, (((1,), (1,)), ((), ())), preferred_element_type=F32)


def dot_tn(a, b):
    return lax.dot_general(a, b, (((0,), (0,)), ((), ())), preferred_element_type=F32)


def sigmoid(v):
    return 0.5 * jnp.tanh(0.5 * v) + 0.5


def stats(v):
    center = jnp.mean(v, axis=0, keepdims=True)
    shifted = v - center
    inv = lax.rsqrt(jnp.mean(shifted * shifted, axis=0, keepdims=True) + 1e-05)
    return shifted * inv, inv


def kernel(
    n_dp, n_ax, factor,
    pair_h, cot_h, w_in_h, w_out_h, gain_in_h, gain_x_h,
    upd_h, gpair_h, gw_in_h, gw_out_h, ggi_h, ggx_h,
    pair, cot, w_in, w_out, gain_in, gain_x,
    upd, gpair, gw_in, gw_out, ggi, ggx, isem, osem, gproj,
    send, recv, tbuf, tbuf2, lc, rc, gc,
    normed, unit_in, inv_in, gate_a, q_a, gate_b, q_b, gate_o, s_x, c_g, glift, xnorm, gnorm,
    w_t, wo_t, gin, gx, dw, r1, r2, s1, s2, fin,
    ssem, rsem, lsem, asend, arecv,
):
    me = lax.axis_index("axial")
    dp = lax.axis_index("dp")
    my_z, my_y, my_c = me // 4, (me // 2) % 2, me % 2

    def peer(o):
        return ((my_z + o // 4) % 4) * 4 + ((my_y + (o // 2) % 2) % 2) * 2 + (my_c + o % 2) % 2

    def dp_peer(o):
        return (dp + o) % n_dp

    def each(lo, hi, fn, unroll=1):
        def body(i, carry):
            fn(i)
            return carry
        lax.fori_loop(lo, hi, body, 0, unroll=unroll)

    barrier = pltpu.get_barrier_semaphore()
    each(1, n_ax, lambda o: pl.semaphore_signal(
        barrier, inc=1, device_id=(dp, peer(o)), device_id_type=MESH))
    each(1, n_dp, lambda o: pl.semaphore_signal(
        barrier, inc=1, device_id=(dp_peer(o), me), device_id_type=MESH))

    half = pl.ds(0, 8), pl.ds(8, 8)
    in_pairs = {
        "w_in": (w_in_h, w_in), "gain_in": (gain_in_h, gain_in),
        "pair0": (pair_h.at[half[0]], pair.at[half[0]]), "pair1": (pair_h.at[half[1]], pair.at[half[1]]),
        "w_out": (w_out_h, w_out), "gain_x": (gain_x_h, gain_x), "cot": (cot_h, cot),
    }
    out_pairs = {
        "upd": (upd, upd_h),
        "gpair0": (gpair.at[half[0]], gpair_h.at[half[0]]), "gpair1": (gpair.at[half[1]], gpair_h.at[half[1]]),
        "gw_in": (gw_in, gw_in_h), "gw_out": (gw_out, gw_out_h), "ggi": (ggi, ggi_h), "ggx": (ggx, ggx_h),
    }
    in_names, put_names = list(in_pairs), list(out_pairs)

    def in_copy(name):
        return pltpu.make_async_copy(*in_pairs[name], isem.at[in_names.index(name)])

    def out_copy(name):
        return pltpu.make_async_copy(*out_pairs[name], osem.at[put_names.index(name)])

    def fetch(name):
        in_copy(name).wait()

    def put_out(name):
        out_copy(name).start()

    for name in in_names:
        in_copy(name).start()

    def start(t):
        def one(o):
            d = peer(o)
            pltpu.make_async_remote_copy(
                src_ref=send.at[t, d], dst_ref=recv.at[t, me],
                send_sem=ssem.at[t], recv_sem=rsem.at[t],
                device_id=(dp, d), device_id_type=MESH).start()
        each(1, n_ax, one)
        pltpu.make_async_copy(send.at[t, me], recv.at[t, me], lsem.at[t]).start()

    def wait_recv(t):
        pltpu.make_async_copy(send.at[t, me], recv.at[t, me], lsem.at[t]).wait()
        part = recv.at[t, pl.ds(0, n_ax - 1)]
        pltpu.make_async_copy(part, part, rsem.at[t]).wait()

    def wait_send(t):
        part = send.at[t, pl.ds(0, n_ax - 1)]
        pltpu.make_async_copy(part, part, ssem.at[t]).wait()

    def reduce_start(p):
        def one(o):
            d = peer(o)
            pltpu.make_async_remote_copy(
                src_ref=dw.at[p, pl.ds(8 * d, 8)], dst_ref=r1.at[p, me],
                send_sem=asend.at[p], recv_sem=arecv.at[p],
                device_id=(dp, d), device_id_type=MESH).start()
        each(1, n_ax, one)
        r1[p, me] = dw[p, pl.ds(8 * me, 8)]

    def reduce_dp(p):
        part = r1.at[p, pl.ds(0, n_ax - 1)]
        pltpu.make_async_copy(part, part, arecv.at[p]).wait()
        total = jnp.sum(r1[p], axis=0)
        s1[p] = total
        r2[p, dp] = total

        def one(o):
            pltpu.make_async_remote_copy(
                src_ref=s1.at[p], dst_ref=r2.at[p, dp],
                send_sem=asend.at[3 + p], recv_sem=arecv.at[3 + p],
                device_id=(dp_peer(o), me), device_id_type=MESH).start()
        each(1, n_dp, one)

    def reduce_back(p):
        part = r2.at[p, pl.ds(0, n_dp - 1)]
        pltpu.make_async_copy(part, part, arecv.at[3 + p]).wait()
        total = jnp.sum(r2[p], axis=0) * factor
        s2[p] = total
        fin[p, me] = total

        def one(o):
            pltpu.make_async_remote_copy(
                src_ref=s2.at[p], dst_ref=fin.at[p, me],
                send_sem=asend.at[6 + p], recv_sem=arecv.at[6 + p],
                device_id=(dp, peer(o)), device_id_type=MESH).start()
        each(1, n_ax, one)

    def reduce_end(p):
        part = fin.at[p, pl.ds(0, n_ax - 1)]
        pltpu.make_async_copy(part, part, arecv.at[6 + p]).wait()

    def reduce_sent(p):
        part = r1.at[p, pl.ds(0, n_ax - 1)]
        pltpu.make_async_copy(part, part, asend.at[p]).wait()
        part = r2.at[p, pl.ds(0, n_dp - 1)]
        pltpu.make_async_copy(part, part, asend.at[3 + p]).wait()
        part = fin.at[p, pl.ds(0, n_ax - 1)]
        pltpu.make_async_copy(part, part, asend.at[6 + p]).wait()

    def strided(i):
        return pl.ds(i, 128, stride=8)

    def put(k, values):
        tbuf2[0, strided(k), :] = values[:, :128]
        tbuf2[1, strided(k), :] = values[:, 128:]

    def take(k):
        return jnp.concatenate([tbuf[0, strided(k), :], tbuf[1, strided(k), :]], axis=1)

    def flush(t):
        for n in range(2):
            send[t, :, :, 128 * n:128 * (n + 1)] = tbuf2[n].astype(BF16).reshape(16, 64, 128)

    def unpack(t):
        for n in range(2):
            tbuf[n] = recv[t, :, :, 128 * n:128 * (n + 1)].astype(F32).reshape(1024, 128)

    def load_pair(t, cp):
        both = recv[t, :, pl.ds(pl.multiple_of(16 * cp, 16), 16), :].astype(F32).reshape(16, 2, 8, 256)
        return both[:, 0], both[:, 1]

    def store_pair(t, cp, even, odd):
        both = jnp.concatenate([even, odd], axis=1).astype(BF16)
        send[t, :, pl.ds(pl.multiple_of(16 * cp, 16), 16), :] = both

    fetch("w_in")
    w_t[...] = w_in[...].astype(F32).T.astype(BF16)
    fetch("gain_in")
    gin[...] = jnp.broadcast_to(jnp.broadcast_to(gain_in[...], (128, 128)).T[:, :1], (128, 256))

    def norm_in(i):
        unit, inv = stats(pair[i].astype(F32).T)
        unit_in[i] = unit
        inv_in[i] = inv
        normed[i] = (unit * gin[...]).astype(BF16)

    def gated(i, k, lo, gate_ref, q_ref):
        projected = dot(w_t[lo:lo + 256], normed[i])
        gate = sigmoid(projected[128:])
        value = projected[:128] * gate
        gate_ref[i] = gate
        q_ref[i] = value * (1.0 - gate)
        put(k, value)

    def first_left(k):
        norm_in(k)
        gated(k, k, 0, gate_a, q_a)

    def first_right(k):
        gated(k, k, 256, gate_b, q_b)

    def second_right(k):
        norm_in(8 + k)
        gated(8 + k, k, 256, gate_b, q_b)

    def second_left(k):
        gated(8 + k, k, 0, gate_a, q_a)

    fetch("pair0")
    each(0, 8, first_left)
    flush(2 * LEFT)
    pl.semaphore_wait(barrier, n_ax - 1 + n_dp - 1)
    start(2 * LEFT)
    each(0, 8, first_right)
    flush(2 * RIGHT)
    start(2 * RIGHT)
    fetch("pair1")
    each(0, 8, second_right)
    flush(2 * RIGHT + 1)
    start(2 * RIGHT + 1)
    each(0, 8, second_left)
    flush(2 * LEFT + 1)
    start(2 * LEFT + 1)

    fetch("w_out")
    fetch("gain_x")
    fetch("cot")
    wo_t[...] = w_out[...].astype(F32).T.astype(BF16)
    gx[...] = jnp.broadcast_to(jnp.broadcast_to(gain_x[...], (128, 128)).T[:, :1], (128, 256))

    def gate_row(i):
        gate = sigmoid(dot(w_t[512:640], normed[i]))
        upstream = cot[i].astype(F32).T
        lift = upstream * gate
        gate_o[i] = gate
        c_g[i] = lift * (1.0 - gate)
        lift = lift.astype(BF16)
        glift[i] = lift
        s_x[i] = dot(w_out[...], lift) * gx[...]
    each(0, 16, gate_row)
    dw[...] = jnp.zeros_like(dw)

    wait_recv(2 * LEFT)
    wait_recv(2 * RIGHT)
    wait_recv(2 * RIGHT + 1)
    for h in range(2):
        if h == 1:
            wait_recv(2 * LEFT + 1)

        def product_pair(cp):
            lefts = load_pair(2 * LEFT + h, cp)
            if h == 0:
                right0, right1 = load_pair(2 * RIGHT, cp), load_pair(2 * RIGHT + 1, cp)
            prods = []
            for e in range(2):
                left = lefts[e].reshape(128, 256).astype(BF16)
                lc[2 * cp + e, 128 * h:128 * (h + 1)] = left
                if h == 0:
                    right = jnp.concatenate([right0[e], right1[e]], axis=1).reshape(256, 256).astype(BF16)
                    rc[2 * cp + e] = right
                else:
                    right = rc[2 * cp + e]
                prods.append(dot_nt(left, right).reshape(16, 8, 256))
            store_pair(2 * PROD + h, cp, prods[0], prods[1])
        each(0, 4, product_pair)
        start(2 * PROD + h)

    for h in range(2):
        wait_recv(2 * PROD + h)
        unpack(2 * PROD + h)

        def norm_row(k):
            i = 8 * h + k
            unit, inv = stats(take(k))
            xnorm[i] = (unit * gx[...]).astype(BF16)
            scaled = s_x[i]
            mean_one = jnp.mean(scaled, axis=0, keepdims=True)
            mean_two = jnp.mean(scaled * unit, axis=0, keepdims=True)
            put(k, (scaled - mean_one - unit * mean_two) * inv)
        each(0, 8, norm_row)
        flush(2 * GPROD + h)
        start(2 * GPROD + h)

    def lift_row(i):
        flat = xnorm[i]
        lifted = dot(wo_t[...], flat)
        upd[i] = (gate_o[i] * lifted).T.astype(BF16)
        ggate = (lifted * c_g[i]).astype(BF16)
        dw[0, :, 0:128] += dot_nt(flat, glift[i])
        dw[0, :, 128:256] += dot_nt(normed[i], ggate)
        gnorm[i] = dot(w_in[:, 512:640], ggate)

    for h in range(2):
        wait_recv(2 * GPROD + h)

        def gleft_pair(cp):
            grads = load_pair(2 * GPROD + h, cp)
            outs = []
            for e in range(2):
                grad = grads[e].reshape(128, 256).astype(BF16)
                gc[2 * cp + e, 128 * h:128 * (h + 1)] = grad
                outs.append(dot(grad, rc[2 * cp + e]).reshape(16, 8, 256))
            store_pair(2 * GLEFT + h, cp, outs[0], outs[1])
        each(0, 4, gleft_pair)
        start(2 * GLEFT + h)
        each(8 * h, 8 * h + 8, lift_row)

    reduce_start(0)

    def gright_pair(cp):
        outs = [dot_tn(gc[2 * cp + e], lc[2 * cp + e]).reshape(16, 2, 8, 256) for e in range(2)]
        for h in range(2):
            store_pair(2 * GRIGHT + h, cp, outs[0][:, h], outs[1][:, h])
    each(0, 4, gright_pair)
    start(2 * GRIGHT)
    start(2 * GRIGHT + 1)
    put_out("upd")

    def back_row(k, h, p, gate_ref, q_ref):
        i = 8 * h + k
        grad = take(k)
        both = jnp.concatenate([grad * gate_ref[i], grad * q_ref[i]], axis=0).astype(BF16)
        gproj[k] = both
        dw[p] += dot_nt(normed[i], both)

    def back_a(h):
        def grad_row(k):
            back_row(k, h, 1, gate_a, q_a)
            gnorm[8 * h + k] += dot(w_in[:, 0:256], gproj[k])
        wait_recv(2 * GLEFT + h)
        unpack(2 * GLEFT + h)
        each(0, 8, grad_row)

    def back_b(h):
        def grad_row(k):
            back_row(k, h, 2, gate_b, q_b)
        wait_recv(2 * GRIGHT + h)
        unpack(2 * GRIGHT + h)
        each(0, 8, grad_row)

    def out_rows(h):
        def out_row(k):
            i = 8 * h + k
            unit = unit_in[i]
            scaled = (gnorm[i] + dot(w_in[:, 256:512], gproj[k])) * gin[...]
            mean_one = jnp.mean(scaled, axis=0, keepdims=True)
            mean_two = jnp.mean(scaled * unit, axis=0, keepdims=True)
            gpair[i] = ((scaled - mean_one - unit * mean_two) * inv_in[i]).T.astype(BF16)
        each(0, 8, out_row)
        put_out("gpair%d" % h)

    back_a(0)
    back_a(1)
    reduce_start(1)
    back_b(0)
    reduce_dp(0)
    out_rows(0)
    back_b(1)
    reduce_start(2)
    reduce_dp(1)
    out_rows(1)
    reduce_dp(2)
    reduce_back(0)
    reduce_back(1)
    reduce_end(0)
    reduce_end(1)
    first = fin[0].reshape(128, 256)
    gw_out[...] = first[:, :128]
    gw_in[:, 512:640] = first[:, 128:]
    gw_in[:, 0:256] = fin[1].reshape(128, 256)
    row_x = jnp.sum(first[:, :128] * w_out[...].astype(F32), axis=1, keepdims=True)
    ggx[...] = jnp.broadcast_to(row_x, (128, 128)).T[:1] / gain_x[...]
    reduce_back(2)
    for t in range(12):
        wait_send(t)
    for p in range(3):
        reduce_sent(p)
    reduce_end(2)
    gw_in[:, 256:512] = fin[2].reshape(128, 256)
    row_in = jnp.sum(gw_in[...] * w_in[...].astype(F32), axis=1, keepdims=True)
    ggi[...] = jnp.broadcast_to(row_in, (128, 128)).T[:1] / gain_in[...]
    for name in ("gw_in", "gw_out", "ggi", "ggx"):
        put_out(name)
    for name in put_names:
        out_copy(name).wait()


def hand_on(*refs):
    n = 6
    sources, targets, held, sems = refs[:n], refs[n:2 * n], refs[2 * n:3 * n], refs[3 * n]
    ins = [pltpu.make_async_copy(sources[k], held[k], sems.at[k]) for k in range(n)]
    outs = [pltpu.make_async_copy(held[k], targets[k], sems.at[n + k]) for k in range(n)]
    for copy in ins:
        copy.start()
    for k in range(n):
        ins[k].wait()
        outs[k].start()
    for copy in outs:
        copy.wait()


def local(n_dp, n_ax, pair, cotangent, in_weight, out_weight, gain_in, gain_x):
    rows, width, chan = pair.shape[1:]
    factor = 1.0 / (n_dp * width * width) ** 0.5
    anywhere = pl.BlockSpec(memory_space=pl.ANY)
    cells = (rows, chan, width)
    args = (pair[0], cotangent[0], in_weight, out_weight, gain_in[None], gain_x[None])
    out_shape = (
        jax.ShapeDtypeStruct((rows, width, chan), BF16),
        jax.ShapeDtypeStruct((rows, width, chan), BF16),
        jax.ShapeDtypeStruct((128, 640), F32),
        jax.ShapeDtypeStruct((128, 128), F32),
        jax.ShapeDtypeStruct((1, 128), F32),
        jax.ShapeDtypeStruct((1, 128), F32),
    )
    outs = pl.pallas_call(
        functools.partial(kernel, n_dp, n_ax, factor),
        name="triangle",
        out_shape=out_shape,
        in_specs=[pl.BlockSpec(memory_space=pltpu.HBM)] * 6,
        out_specs=(anywhere,) * 6,
        scratch_shapes=[pltpu.VMEM(v.shape, v.dtype) for v in args + out_shape] + [
            pltpu.SemaphoreType.DMA((7,)),
            pltpu.SemaphoreType.DMA((7,)),
            pltpu.VMEM((8, 256, 256), BF16),
            pltpu.VMEM((12, 16, 64, 256), BF16),
            pltpu.VMEM((12, 16, 64, 256), BF16),
            pltpu.VMEM((2, 1024, 128), F32),
            pltpu.VMEM((2, 1024, 128), F32),
            pltpu.VMEM((8, 256, 256), BF16),
            pltpu.VMEM((8, 256, 256), BF16),
            pltpu.VMEM((8, 256, 256), BF16),
            pltpu.VMEM(cells, BF16),
            pltpu.VMEM(cells, F32),
            pltpu.VMEM((rows, 1, width), F32),
            pltpu.VMEM(cells, F32),
            pltpu.VMEM(cells, F32),
            pltpu.VMEM(cells, F32),
            pltpu.VMEM(cells, F32),
            pltpu.VMEM(cells, F32),
            pltpu.VMEM(cells, F32),
            pltpu.VMEM(cells, F32),
            pltpu.VMEM(cells, BF16),
            pltpu.VMEM(cells, BF16),
            pltpu.VMEM(cells, F32),
            pltpu.VMEM((640, 128), BF16),
            pltpu.VMEM((128, 128), BF16),
            pltpu.VMEM((128, 256), F32),
            pltpu.VMEM((128, 256), F32),
            pltpu.VMEM((3, 128, 256), F32),
            pltpu.VMEM((3, 16, 8, 256), F32),
            pltpu.VMEM((3, 8, 8, 256), F32),
            pltpu.VMEM((3, 8, 256), F32),
            pltpu.VMEM((3, 8, 256), F32),
            pltpu.VMEM((3, 16, 8, 256), F32),
            pltpu.SemaphoreType.DMA((12,)),
            pltpu.SemaphoreType.DMA((12,)),
            pltpu.SemaphoreType.DMA((12,)),
            pltpu.SemaphoreType.DMA((9,)),
            pltpu.SemaphoreType.DMA((9,)),
        ],
        compiler_params=pltpu.CompilerParams(
            collective_id=0, has_side_effects=True, vmem_limit_bytes=60 * 2**20),
        cost_estimate=pl.CostEstimate(
            flops=3_300_000_000, bytes_accessed=5_000_000, transcendentals=1_600_000),
    )(*args)
    upd, gpair, gw_in, gw_out, ggi, ggx = pl.pallas_call(
        hand_on,
        name="hand_on",
        out_shape=out_shape,
        in_specs=[anywhere] * 6,
        out_specs=(anywhere,) * 6,
        scratch_shapes=[pltpu.VMEM(v.shape, v.dtype) for v in out_shape] + [
            pltpu.SemaphoreType.DMA((12,))],
        compiler_params=pltpu.CompilerParams(vmem_limit_bytes=60 * 2**20),
    )(*outs)
    return upd[None], gpair[None], gw_in, gw_out, ggi[0], ggx[0]


def solution(mesh):
    cells = P("dp", "axial", None, None)
    n_dp, n_ax = mesh.shape["dp"], mesh.shape["axial"]
    return jax.shard_map(
        functools.partial(local, n_dp, n_ax), mesh=mesh,
        in_specs=(cells, cells, P(), P(), P(), P()),
        out_specs=(cells, cells, P(), P(), P(), P()), check_vma=False)
```

```python
import functools

import jax
import jax.numpy as jnp
from jax import lax
from jax.experimental import pallas as pl
from jax.experimental.pallas import tpu as pltpu
from jax.sharding import PartitionSpec as P

MESH = pl.DeviceIdType.MESH
F32 = jnp.float32
BF16 = jnp.bfloat16
UNROLL = 2
LEFT, RIGHT, PROD, GPROD, GLEFT, GRIGHT = range(6)


def dot(a, b):
    return lax.dot_general(a, b, (((1,), (0,)), ((), ())), preferred_element_type=F32)


def dot_nt(a, b):
    return lax.dot_general(a, b, (((1,), (1,)), ((), ())), preferred_element_type=F32)


def dot_tn(a, b):
    return lax.dot_general(a, b, (((0,), (0,)), ((), ())), preferred_element_type=F32)


def sigmoid(v):
    return 0.5 * jnp.tanh(0.5 * v) + 0.5


def stats(v):
    center = jnp.mean(v, axis=0, keepdims=True)
    shifted = v - center
    inv = lax.rsqrt(jnp.mean(shifted * shifted, axis=0, keepdims=True) + 1e-05)
    return shifted * inv, inv


def kernel(
    n_dp, n_ax, factor,
    pair_h, cot_h, w_in_h, w_out_h, gain_in_h, gain_x_h,
    upd_h, gpair_h, fin,
    pair, cot, w_in, w_out, gain_in, gain_x,
    upd, gpair, isem, osem, fsem, gproj,
    send, recv, tbuf, tbuf2, lc, rc, gc,
    normed, unit_in, inv_in, gate_a, q_a, gate_b, q_b, gate_o, s_x, c_g, glift, xnorm, gnorm,
    w_t, wo_t, gin, gx, dw, r1, r2, s1, s2,
    ssem, rsem, lsem, asend, arecv,
):
    me = lax.axis_index("axial")
    dp = lax.axis_index("dp")
    my_z, my_y, my_c = me // 4, (me // 2) % 2, me % 2

    def peer(o):
        return ((my_z + o // 4) % 4) * 4 + ((my_y + (o // 2) % 2) % 2) * 2 + (my_c + o % 2) % 2

    def dp_peer(o):
        return (dp + o) % n_dp

    def each(lo, hi, fn, unroll=UNROLL):
        def body(i, carry):
            fn(i)
            return carry
        lax.fori_loop(lo, hi, body, 0, unroll=unroll)

    barrier = pltpu.get_barrier_semaphore()
    each(1, n_ax, lambda o: pl.semaphore_signal(
        barrier, inc=1, device_id=(dp, peer(o)), device_id_type=MESH))
    each(1, n_dp, lambda o: pl.semaphore_signal(
        barrier, inc=1, device_id=(dp_peer(o), me), device_id_type=MESH))

    half = pl.ds(0, 8), pl.ds(8, 8)
    in_pairs = {
        "w_in": (w_in_h, w_in), "gain_in": (gain_in_h, gain_in),
        "pair0": (pair_h.at[half[0]], pair.at[half[0]]), "pair1": (pair_h.at[half[1]], pair.at[half[1]]),
        "w_out": (w_out_h, w_out), "gain_x": (gain_x_h, gain_x), "cot": (cot_h, cot),
    }
    out_pairs = {
        "upd": (upd, upd_h),
        "gpair0": (gpair.at[half[0]], gpair_h.at[half[0]]), "gpair1": (gpair.at[half[1]], gpair_h.at[half[1]]),
    }
    in_names, put_names = list(in_pairs), list(out_pairs)

    def in_copy(name):
        return pltpu.make_async_copy(*in_pairs[name], isem.at[in_names.index(name)])

    def out_copy(name):
        return pltpu.make_async_copy(*out_pairs[name], osem.at[put_names.index(name)])

    def fetch(name):
        in_copy(name).wait()

    def put_out(name):
        out_copy(name).start()

    for name in in_names:
        in_copy(name).start()

    def start(t):
        def one(o):
            d = peer(o)
            pltpu.make_async_remote_copy(
                src_ref=send.at[t, d], dst_ref=recv.at[t, me],
                send_sem=ssem.at[t], recv_sem=rsem.at[t],
                device_id=(dp, d), device_id_type=MESH).start()
        each(1, n_ax, one)
        pltpu.make_async_copy(send.at[t, me], recv.at[t, me], lsem.at[t]).start()

    def wait_recv(t):
        pltpu.make_async_copy(send.at[t, me], recv.at[t, me], lsem.at[t]).wait()
        part = recv.at[t, pl.ds(0, n_ax - 1)]
        pltpu.make_async_copy(part, part, rsem.at[t]).wait()

    def wait_send(t):
        part = send.at[t, pl.ds(0, n_ax - 1)]
        pltpu.make_async_copy(part, part, ssem.at[t]).wait()

    def reduce_start(p):
        def one(o):
            d = peer(o)
            pltpu.make_async_remote_copy(
                src_ref=dw.at[p, pl.ds(8 * d, 8)], dst_ref=r1.at[p, me],
                send_sem=asend.at[p], recv_sem=arecv.at[p],
                device_id=(dp, d), device_id_type=MESH).start()
        each(1, n_ax, one)
        r1[p, me] = dw[p, pl.ds(8 * me, 8)]

    def reduce_dp(p):
        part = r1.at[p, pl.ds(0, n_ax - 1)]
        pltpu.make_async_copy(part, part, arecv.at[p]).wait()
        total = jnp.sum(r1[p], axis=0)
        s1[p] = total
        r2[p, dp] = total

        def one(o):
            pltpu.make_async_remote_copy(
                src_ref=s1.at[p], dst_ref=r2.at[p, dp],
                send_sem=asend.at[3 + p], recv_sem=arecv.at[3 + p],
                device_id=(dp_peer(o), me), device_id_type=MESH).start()
        each(1, n_dp, one)

    def reduce_back(p):
        part = r2.at[p, pl.ds(0, n_dp - 1)]
        pltpu.make_async_copy(part, part, arecv.at[3 + p]).wait()
        total = jnp.sum(r2[p], axis=0) * factor
        s2[p] = total
        pltpu.make_async_copy(s2.at[p], fin.at[p, me], fsem.at[p]).start()

        def one(o):
            pltpu.make_async_remote_copy(
                src_ref=s2.at[p], dst_ref=fin.at[p, me],
                send_sem=asend.at[6 + p], recv_sem=arecv.at[6 + p],
                device_id=(dp, peer(o)), device_id_type=MESH).start()
        each(1, n_ax, one)

    def reduce_end(p):
        part = fin.at[p, pl.ds(0, n_ax - 1)]
        pltpu.make_async_copy(part, part, arecv.at[6 + p]).wait()
        pltpu.make_async_copy(s2.at[p], fin.at[p, me], fsem.at[p]).wait()

    def reduce_sent(p):
        part = r1.at[p, pl.ds(0, n_ax - 1)]
        pltpu.make_async_copy(part, part, asend.at[p]).wait()
        part = r2.at[p, pl.ds(0, n_dp - 1)]
        pltpu.make_async_copy(part, part, asend.at[3 + p]).wait()
        part = fin.at[p, pl.ds(0, n_ax - 1)]
        pltpu.make_async_copy(part, part, asend.at[6 + p]).wait()

    def strided(i):
        return pl.ds(i, 128, stride=8)

    def put(k, values):
        tbuf2[0, strided(k), :] = values[:, :128]
        tbuf2[1, strided(k), :] = values[:, 128:]

    def take(k):
        return jnp.concatenate([tbuf[0, strided(k), :], tbuf[1, strided(k), :]], axis=1)

    def flush(t):
        for n in range(2):
            send[t, :, :, 128 * n:128 * (n + 1)] = tbuf2[n].astype(BF16).reshape(16, 64, 128)

    def unpack(t):
        for n in range(2):
            tbuf[n] = recv[t, :, :, 128 * n:128 * (n + 1)].astype(F32).reshape(1024, 128)

    def load_pair(t, cp):
        both = recv[t, :, pl.ds(pl.multiple_of(16 * cp, 16), 16), :].astype(F32).reshape(16, 2, 8, 256)
        return both[:, 0], both[:, 1]

    def store_pair(t, cp, even, odd):
        both = jnp.concatenate([even, odd], axis=1).astype(BF16)
        send[t, :, pl.ds(pl.multiple_of(16 * cp, 16), 16), :] = both

    fetch("w_in")
    w_t[...] = w_in[...].astype(F32).T.astype(BF16)
    fetch("gain_in")
    gin[...] = jnp.broadcast_to(jnp.broadcast_to(gain_in[...], (128, 128)).T[:, :1], (128, 256))

    def norm_in(i):
        unit, inv = stats(pair[i].astype(F32).T)
        unit_in[i] = unit
        inv_in[i] = inv
        normed[i] = (unit * gin[...]).astype(BF16)

    def gated(i, k, lo, gate_ref, q_ref):
        projected = dot(w_t[lo:lo + 256], normed[i])
        gate = sigmoid(projected[128:])
        value = projected[:128] * gate
        gate_ref[i] = gate
        q_ref[i] = value * (1.0 - gate)
        put(k, value)

    def first_left(k):
        norm_in(k)
        gated(k, k, 0, gate_a, q_a)

    def first_right(k):
        gated(k, k, 256, gate_b, q_b)

    def second_right(k):
        norm_in(8 + k)
        gated(8 + k, k, 256, gate_b, q_b)

    def second_left(k):
        gated(8 + k, k, 0, gate_a, q_a)

    fetch("pair0")
    each(0, 8, first_left)
    flush(2 * LEFT)
    pl.semaphore_wait(barrier, n_ax - 1 + n_dp - 1)
    start(2 * LEFT)
    each(0, 8, first_right)
    flush(2 * RIGHT)
    start(2 * RIGHT)
    fetch("pair1")
    each(0, 8, second_right)
    flush(2 * RIGHT + 1)
    start(2 * RIGHT + 1)
    each(0, 8, second_left)
    flush(2 * LEFT + 1)
    start(2 * LEFT + 1)

    fetch("w_out")
    fetch("gain_x")
    fetch("cot")
    wo_t[...] = w_out[...].astype(F32).T.astype(BF16)
    gx[...] = jnp.broadcast_to(jnp.broadcast_to(gain_x[...], (128, 128)).T[:, :1], (128, 256))

    def gate_row(i):
        gate = sigmoid(dot(w_t[512:640], normed[i]))
        upstream = cot[i].astype(F32).T
        lift = upstream * gate
        gate_o[i] = gate
        c_g[i] = lift * (1.0 - gate)
        lift = lift.astype(BF16)
        glift[i] = lift
        s_x[i] = dot(w_out[...], lift) * gx[...]
    each(0, 16, gate_row)
    dw[...] = jnp.zeros_like(dw)

    wait_recv(2 * LEFT)
    wait_recv(2 * RIGHT)
    wait_recv(2 * RIGHT + 1)
    for h in range(2):
        if h == 1:
            wait_recv(2 * LEFT + 1)

        def product_pair(cp):
            lefts = load_pair(2 * LEFT + h, cp)
            if h == 0:
                right0, right1 = load_pair(2 * RIGHT, cp), load_pair(2 * RIGHT + 1, cp)
            prods = []
            for e in range(2):
                left = lefts[e].reshape(128, 256).astype(BF16)
                lc[2 * cp + e, 128 * h:128 * (h + 1)] = left
                if h == 0:
                    right = jnp.concatenate([right0[e], right1[e]], axis=1).reshape(256, 256).astype(BF16)
                    rc[2 * cp + e] = right
                else:
                    right = rc[2 * cp + e]
                prods.append(dot_nt(left, right).reshape(16, 8, 256))
            store_pair(2 * PROD + h, cp, prods[0], prods[1])
        each(0, 4, product_pair)
        start(2 * PROD + h)

    for h in range(2):
        wait_recv(2 * PROD + h)
        unpack(2 * PROD + h)

        def norm_row(k):
            i = 8 * h + k
            unit, inv = stats(take(k))
            xnorm[i] = (unit * gx[...]).astype(BF16)
            scaled = s_x[i]
            mean_one = jnp.mean(scaled, axis=0, keepdims=True)
            mean_two = jnp.mean(scaled * unit, axis=0, keepdims=True)
            put(k, (scaled - mean_one - unit * mean_two) * inv)
        each(0, 8, norm_row)
        flush(2 * GPROD + h)
        start(2 * GPROD + h)

    def lift_row(i):
        flat = xnorm[i]
        lifted = dot(wo_t[...], flat)
        upd[i] = (gate_o[i] * lifted).T.astype(BF16)
        ggate = (lifted * c_g[i]).astype(BF16)
        dw[0, :, 0:128] += dot_nt(flat, glift[i])
        dw[0, :, 128:256] += dot_nt(normed[i], ggate)
        gnorm[i] = dot(w_in[:, 512:640], ggate)

    for h in range(2):
        wait_recv(2 * GPROD + h)

        def gleft_pair(cp):
            grads = load_pair(2 * GPROD + h, cp)
            outs = []
            for e in range(2):
                grad = grads[e].reshape(128, 256).astype(BF16)
                gc[2 * cp + e, 128 * h:128 * (h + 1)] = grad
                outs.append(dot(grad, rc[2 * cp + e]).reshape(16, 8, 256))
            store_pair(2 * GLEFT + h, cp, outs[0], outs[1])
        each(0, 4, gleft_pair)
        start(2 * GLEFT + h)
        each(8 * h, 8 * h + 8, lift_row)

    reduce_start(0)

    def gright_pair(cp):
        outs = [dot_tn(gc[2 * cp + e], lc[2 * cp + e]).reshape(16, 2, 8, 256) for e in range(2)]
        for h in range(2):
            store_pair(2 * GRIGHT + h, cp, outs[0][:, h], outs[1][:, h])
    each(0, 4, gright_pair)
    start(2 * GRIGHT)
    start(2 * GRIGHT + 1)
    put_out("upd")

    def back_a(h):
        def grad_row(k):
            i = 8 * h + k
            grad = take(k)
            both = jnp.concatenate([grad * gate_a[i], grad * q_a[i]], axis=0).astype(BF16)
            dw[1] += dot_nt(normed[i], both)
            gnorm[i] += dot(w_in[:, 0:256], both)
        wait_recv(2 * GLEFT + h)
        unpack(2 * GLEFT + h)
        each(0, 8, grad_row)

    def back_b(h):
        wait_recv(2 * GRIGHT + h)
        unpack(2 * GRIGHT + h)
        total = dw[2]
        for k in range(8):
            i = 8 * h + k
            grad = take(k)
            both = jnp.concatenate([grad * gate_b[i], grad * q_b[i]], axis=0).astype(BF16)
            gproj[k] = both
            total += dot_nt(normed[i], both)
        dw[2] = total

    def out_rows(h):
        def out_row(k):
            i = 8 * h + k
            unit = unit_in[i]
            scaled = (gnorm[i] + dot(w_in[:, 256:512], gproj[k])) * gin[...]
            mean_one = jnp.mean(scaled, axis=0, keepdims=True)
            mean_two = jnp.mean(scaled * unit, axis=0, keepdims=True)
            gpair[i] = ((scaled - mean_one - unit * mean_two) * inv_in[i]).T.astype(BF16)
        each(0, 8, out_row)
        put_out("gpair%d" % h)

    back_a(0)
    back_a(1)
    reduce_start(1)
    back_b(0)
    reduce_dp(0)
    out_rows(0)
    back_b(1)
    reduce_start(2)
    reduce_dp(1)
    reduce_back(0)
    out_rows(1)
    reduce_dp(2)
    reduce_back(1)
    reduce_back(2)
    for t in range(12):
        wait_send(t)
    for name in put_names:
        out_copy(name).wait()
    for p in range(3):
        reduce_sent(p)
    for p in range(3):
        reduce_end(p)


def hand_on(
    upd_h, gpair_h, fin_h, w_in_h, w_out_h, gain_in_h, gain_x_h,
    upd_o, gpair_o, gw_in_o, gw_out_o, ggi_o, ggx_o,
    upd, gpair, gw_in, gw_out, ggi, ggx, fin, w_in, w_out, gain_in, gain_x, isem, osem,
):
    def moves(pairs, sems, first):
        return [pltpu.make_async_copy(a, b, sems.at[first + n]) for n, (a, b) in enumerate(pairs)]

    small_in = moves(((fin_h, fin), (w_in_h, w_in), (w_out_h, w_out), (gain_in_h, gain_in),
                      (gain_x_h, gain_x)), isem, 0)
    big_in = moves(((upd_h, upd), (gpair_h, gpair)), isem, 5)
    big_out = moves(((upd, upd_o), (gpair, gpair_o)), osem, 0)
    small_out = moves(((gw_in, gw_in_o), (gw_out, gw_out_o), (ggi, ggi_o), (ggx, ggx_o)), osem, 2)
    for copy in small_in + big_in:
        copy.start()
    for copy in small_in:
        copy.wait()
    gw_out[...] = fin[0, :, 0:128]
    gw_in[:, 512:640] = fin[0, :, 128:256]
    gw_in[:, 0:256] = fin[1]
    gw_in[:, 256:512] = fin[2]
    small_out[0].start()
    small_out[1].start()
    for n in range(2):
        big_in[n].wait()
        big_out[n].start()
    row_x = jnp.sum(gw_out[...] * w_out[...].astype(F32), axis=1, keepdims=True)
    ggx[...] = jnp.broadcast_to(row_x, (128, 128)).T[:1] / gain_x[...]
    row_in = jnp.sum(gw_in[...] * w_in[...].astype(F32), axis=1, keepdims=True)
    ggi[...] = jnp.broadcast_to(row_in, (128, 128)).T[:1] / gain_in[...]
    small_out[2].start()
    small_out[3].start()
    for copy in big_out + small_out:
        copy.wait()


def local(n_dp, n_ax, pair, cotangent, in_weight, out_weight, gain_in, gain_x):
    rows, width, chan = pair.shape[1:]
    factor = 1.0 / (n_dp * width * width) ** 0.5
    anywhere = pl.BlockSpec(memory_space=pl.ANY)
    cells = (rows, chan, width)
    args = (pair[0], cotangent[0], in_weight, out_weight, gain_in[None], gain_x[None])
    out_shape = (
        jax.ShapeDtypeStruct((rows, width, chan), BF16),
        jax.ShapeDtypeStruct((rows, width, chan), BF16),
        jax.ShapeDtypeStruct((128, 640), F32),
        jax.ShapeDtypeStruct((128, 128), F32),
        jax.ShapeDtypeStruct((1, 128), F32),
        jax.ShapeDtypeStruct((1, 128), F32),
    )
    sums_shape = jax.ShapeDtypeStruct((3, 16, 8, 256), F32)
    upd, gpair, sums = pl.pallas_call(
        functools.partial(kernel, n_dp, n_ax, factor),
        name="triangle",
        out_shape=out_shape[:2] + (sums_shape,),
        in_specs=[anywhere] * 6,
        out_specs=(anywhere,) * 3,
        scratch_shapes=[pltpu.VMEM(v.shape, v.dtype) for v in args + out_shape[:2]] + [
            pltpu.SemaphoreType.DMA((7,)),
            pltpu.SemaphoreType.DMA((3,)),
            pltpu.SemaphoreType.DMA((3,)),
            pltpu.VMEM((8, 256, 256), BF16),
            pltpu.VMEM((12, 16, 64, 256), BF16),
            pltpu.VMEM((12, 16, 64, 256), BF16),
            pltpu.VMEM((2, 1024, 128), F32),
            pltpu.VMEM((2, 1024, 128), F32),
            pltpu.VMEM((8, 256, 256), BF16),
            pltpu.VMEM((8, 256, 256), BF16),
            pltpu.VMEM((8, 256, 256), BF16),
            pltpu.VMEM(cells, BF16),
            pltpu.VMEM(cells, F32),
            pltpu.VMEM((rows, 1, width), F32),
            pltpu.VMEM(cells, F32),
            pltpu.VMEM(cells, F32),
            pltpu.VMEM(cells, F32),
            pltpu.VMEM(cells, F32),
            pltpu.VMEM(cells, F32),
            pltpu.VMEM(cells, F32),
            pltpu.VMEM(cells, F32),
            pltpu.VMEM(cells, BF16),
            pltpu.VMEM(cells, BF16),
            pltpu.VMEM(cells, F32),
            pltpu.VMEM((640, 128), BF16),
            pltpu.VMEM((128, 128), BF16),
            pltpu.VMEM((128, 256), F32),
            pltpu.VMEM((128, 256), F32),
            pltpu.VMEM((3, 128, 256), F32),
            pltpu.VMEM((3, 16, 8, 256), F32),
            pltpu.VMEM((3, 8, 8, 256), F32),
            pltpu.VMEM((3, 8, 256), F32),
            pltpu.VMEM((3, 8, 256), F32),
            pltpu.SemaphoreType.DMA((12,)),
            pltpu.SemaphoreType.DMA((12,)),
            pltpu.SemaphoreType.DMA((12,)),
            pltpu.SemaphoreType.DMA((9,)),
            pltpu.SemaphoreType.DMA((9,)),
        ],
        compiler_params=pltpu.CompilerParams(
            collective_id=0, has_side_effects=True, vmem_limit_bytes=60 * 2**20),
        cost_estimate=pl.CostEstimate(
            flops=3_300_000_000, bytes_accessed=5_000_000, transcendentals=1_600_000),
    )(*args)
    upd, gpair, gw_in, gw_out, ggi, ggx = pl.pallas_call(
        hand_on,
        name="hand_on",
        out_shape=out_shape,
        in_specs=[anywhere] * 7,
        out_specs=(anywhere,) * 6,
        scratch_shapes=[pltpu.VMEM(v.shape, v.dtype) for v in out_shape] + [
            pltpu.VMEM((3, 128, 256), F32)] + [pltpu.VMEM(v.shape, v.dtype) for v in args[2:]] + [
            pltpu.SemaphoreType.DMA((7,)),
            pltpu.SemaphoreType.DMA((6,)),
        ],
        compiler_params=pltpu.CompilerParams(vmem_limit_bytes=60 * 2**20),
    )(upd, gpair, sums.reshape(3, 128, 256), *args[2:])
    return upd[None], gpair[None], gw_in, gw_out, ggi[0], ggx[0]


def solution(mesh):
    cells = P("dp", "axial", None, None)
    n_dp, n_ax = mesh.shape["dp"], mesh.shape["axial"]
    return jax.shard_map(
        functools.partial(local, n_dp, n_ax), mesh=mesh,
        in_specs=(cells, cells, P(), P(), P(), P()),
        out_specs=(cells, cells, P(), P(), P(), P()), check_vma=False)
```

```python
import functools

import jax
import jax.numpy as jnp
from jax import lax
from jax.experimental import pallas as pl
from jax.experimental.pallas import tpu as pltpu
from jax.sharding import PartitionSpec as P

MESH = pl.DeviceIdType.MESH
F32 = jnp.float32
BF16 = jnp.bfloat16
UNROLL = 2
LEFT, RIGHT, PROD, GPROD, GLEFT, GRIGHT = range(6)


def dot(a, b):
    return lax.dot_general(a, b, (((1,), (0,)), ((), ())), preferred_element_type=F32)


def dot_nt(a, b):
    return lax.dot_general(a, b, (((1,), (1,)), ((), ())), preferred_element_type=F32)


def dot_tn(a, b):
    return lax.dot_general(a, b, (((0,), (0,)), ((), ())), preferred_element_type=F32)


def sigmoid(v):
    return 0.5 * jnp.tanh(0.5 * v) + 0.5


def stats(v):
    center = jnp.mean(v, axis=0, keepdims=True)
    shifted = v - center
    inv = lax.rsqrt(jnp.mean(shifted * shifted, axis=0, keepdims=True) + 1e-05)
    return shifted * inv, inv


def kernel(
    n_dp, n_ax, factor,
    pair_h, cot_h, w_in_h, w_out_h, gain_in_h, gain_x_h,
    upd_h, gpair_h, fin,
    pair, cot, w_in, w_out, gain_in, gain_x,
    upd, gpair, isem, osem, fsem, gproj,
    send, recv, tbuf, tbuf2, lc, rc, gc,
    normed, unit_in, inv_in, gate_a, q_a, gate_b, q_b, gate_o, s_x, c_g, glift, xnorm, gnorm,
    w_t, wo_t, gin, gx, dw, r1, r2, s1, s2, x1, xs, a1, a2, s3, s4, xg,
    ssem, rsem, lsem, asend, arecv,
):
    me = lax.axis_index("axial")
    dp = lax.axis_index("dp")
    my_z, my_y, my_c = me // 4, (me // 2) % 2, me % 2

    def peer(o):
        return ((my_z + o // 4) % 4) * 4 + ((my_y + (o // 2) % 2) % 2) * 2 + (my_c + o % 2) % 2

    def dp_peer(o):
        return (dp + o) % n_dp

    def each(lo, hi, fn, unroll=UNROLL):
        def body(i, carry):
            fn(i)
            return carry
        lax.fori_loop(lo, hi, body, 0, unroll=unroll)

    barrier = pltpu.get_barrier_semaphore()
    each(1, n_ax, lambda o: pl.semaphore_signal(
        barrier, inc=1, device_id=(dp, peer(o)), device_id_type=MESH))
    each(1, n_dp, lambda o: pl.semaphore_signal(
        barrier, inc=1, device_id=(dp_peer(o), me), device_id_type=MESH))

    half = pl.ds(0, 8), pl.ds(8, 8)
    in_pairs = {
        "w_in": (w_in_h, w_in), "gain_in": (gain_in_h, gain_in),
        "pair0": (pair_h.at[half[0]], pair.at[half[0]]), "pair1": (pair_h.at[half[1]], pair.at[half[1]]),
        "w_out": (w_out_h, w_out), "gain_x": (gain_x_h, gain_x), "cot": (cot_h, cot),
    }
    out_pairs = {
        "upd": (upd, upd_h),
        "gpair0": (gpair.at[half[0]], gpair_h.at[half[0]]), "gpair1": (gpair.at[half[1]], gpair_h.at[half[1]]),
    }
    in_names, put_names = list(in_pairs), list(out_pairs)

    def in_copy(name):
        return pltpu.make_async_copy(*in_pairs[name], isem.at[in_names.index(name)])

    def out_copy(name):
        return pltpu.make_async_copy(*out_pairs[name], osem.at[put_names.index(name)])

    def fetch(name):
        in_copy(name).wait()

    def put_out(name):
        out_copy(name).start()

    for name in in_names:
        in_copy(name).start()

    def start(t):
        def one(o):
            d = peer(o)
            pltpu.make_async_remote_copy(
                src_ref=send.at[t, d], dst_ref=recv.at[t, me],
                send_sem=ssem.at[t], recv_sem=rsem.at[t],
                device_id=(dp, d), device_id_type=MESH).start()
        each(1, n_ax, one)
        pltpu.make_async_copy(send.at[t, me], recv.at[t, me], lsem.at[t]).start()

    def wait_recv(t):
        pltpu.make_async_copy(send.at[t, me], recv.at[t, me], lsem.at[t]).wait()
        part = recv.at[t, pl.ds(0, n_ax - 1)]
        pltpu.make_async_copy(part, part, rsem.at[t]).wait()

    def wait_send(t):
        part = send.at[t, pl.ds(0, n_ax - 1)]
        pltpu.make_async_copy(part, part, ssem.at[t]).wait()

    def bytes_of(ref, sem):
        pltpu.make_async_copy(ref, ref, sem).wait()

    def push(src, dst, k, dp_index, ax_index):
        pltpu.make_async_remote_copy(
            src_ref=src, dst_ref=dst, send_sem=asend.at[k], recv_sem=arecv.at[k],
            device_id=(dp_index, ax_index), device_id_type=MESH).start()

    def rows8(n):
        return pl.ds(pl.multiple_of(8 * n, 8), 8)

    def rows32(n):
        return pl.ds(pl.multiple_of(32 * n, 32), 32)

    right_blocks = pl.ds(4, 2)
    others = pl.ds(0, n_ax - 1)

    def right_start():
        def one(o):
            d = peer(o)
            push(dw.at[right_blocks, rows8(d)], r1.at[me], 0, dp, d)
        each(1, n_ax, one)
        r1[me] = dw[4:6, rows8(me)]

    def right_dp():
        bytes_of(r1.at[others], arecv.at[0])
        total = jnp.sum(r1[...], axis=0)
        s1[...] = total
        r2[dp] = total
        each(1, n_dp, lambda o: push(s1, r2.at[dp], 1, dp_peer(o), me))

    def right_back():
        bytes_of(r2.at[pl.ds(0, n_dp - 1)], arecv.at[1])
        s2[...] = jnp.sum(r2[...], axis=0) * factor
        target = fin.at[right_blocks, rows8(me)]
        pltpu.make_async_copy(s2, target, fsem.at[0]).start()
        each(1, n_ax, lambda o: push(s2, target, 2, dp, peer(o)))

    my_x, my_yl = dp % 4, dp // 4

    def x_peer(o):
        return my_yl * 4 + (my_x + o) % 4

    def x_start(p):
        def one(o):
            push(dw.at[pl.ds(2 * p, 2), rows32((my_x + o) % 4)], x1.at[p, my_x], 3 + p, x_peer(o), me)
        each(1, 4, one)
        x1[p, my_x] = dw[2 * p:2 * p + 2, rows32(my_x)]

    def left_axial():
        for p in range(2):
            bytes_of(x1.at[p, pl.ds(0, 3)], arecv.at[3 + p])
            xs[2 * p:2 * p + 2] = jnp.sum(x1[p], axis=0)

        def one(o):
            d = peer(o)
            push(xs.at[d // 4, rows8(d % 4)], a1.at[me], 5, dp, d)
        each(1, n_ax, one)
        a1[me] = xs[me // 4, rows8(me % 4)]

    def left_y():
        bytes_of(a1.at[others], arecv.at[5])
        total = jnp.sum(a1[...], axis=0)
        s3[...] = total
        a2[my_yl] = total
        push(s3, a2.at[my_yl], 6, (dp + 4) % 8, me)

    def left_back():
        bytes_of(a2.at[0], arecv.at[6])
        total = (a2[0] + a2[1]) * factor
        s4[...] = total
        xg[me // 4, rows8(me % 4)] = total
        each(1, n_ax, lambda o: push(s4, xg.at[me // 4, rows8(me % 4)], 7, dp, peer(o)))

    def left_x():
        bytes_of(a1.at[others], arecv.at[7])
        target = fin.at[pl.ds(0, 4), rows32(my_x)]
        pltpu.make_async_copy(xg, target, fsem.at[1]).start()
        each(1, 4, lambda o: push(xg, target, 8, x_peer(o), me))

    def reduce_end():
        for sem in (asend, arecv):
            bytes_of(fin.at[right_blocks, pl.ds(0, 8 * (n_ax - 1))], sem.at[2])
            bytes_of(fin.at[pl.ds(0, 4), pl.ds(0, 96)], sem.at[8])
        bytes_of(r1.at[others], asend.at[0])
        bytes_of(r2.at[pl.ds(0, n_dp - 1)], asend.at[1])
        for p in range(2):
            bytes_of(x1.at[p, pl.ds(0, 3)], asend.at[3 + p])
        bytes_of(a1.at[others], asend.at[5])
        bytes_of(a2.at[0], asend.at[6])
        bytes_of(a1.at[others], asend.at[7])
        pltpu.make_async_copy(s2, fin.at[right_blocks, rows8(me)], fsem.at[0]).wait()
        pltpu.make_async_copy(xg, fin.at[pl.ds(0, 4), rows32(my_x)], fsem.at[1]).wait()

    def strided(i):
        return pl.ds(i, 128, stride=8)

    def put(k, values):
        tbuf2[0, strided(k), :] = values[:, :128]
        tbuf2[1, strided(k), :] = values[:, 128:]

    def take(k):
        return jnp.concatenate([tbuf[0, strided(k), :], tbuf[1, strided(k), :]], axis=1)

    def flush(t):
        for n in range(2):
            send[t, :, :, 128 * n:128 * (n + 1)] = tbuf2[n].astype(BF16).reshape(16, 64, 128)

    def unpack(t):
        for n in range(2):
            tbuf[n] = recv[t, :, :, 128 * n:128 * (n + 1)].astype(F32).reshape(1024, 128)

    def load_pair(t, cp):
        both = recv[t, :, pl.ds(pl.multiple_of(16 * cp, 16), 16), :].astype(F32).reshape(16, 2, 8, 256)
        return both[:, 0], both[:, 1]

    def store_pair(t, cp, even, odd):
        both = jnp.concatenate([even, odd], axis=1).astype(BF16)
        send[t, :, pl.ds(pl.multiple_of(16 * cp, 16), 16), :] = both

    fetch("w_in")
    w_t[...] = w_in[...].astype(F32).T.astype(BF16)
    fetch("gain_in")
    gin[...] = jnp.broadcast_to(jnp.broadcast_to(gain_in[...], (128, 128)).T[:, :1], (128, 256))

    def norm_in(i):
        unit, inv = stats(pair[i].astype(F32).T)
        unit_in[i] = unit
        inv_in[i] = inv
        normed[i] = (unit * gin[...]).astype(BF16)

    def gated(i, k, lo, gate_ref, q_ref):
        projected = dot(w_t[lo:lo + 256], normed[i])
        gate = sigmoid(projected[128:])
        value = projected[:128] * gate
        gate_ref[i] = gate
        q_ref[i] = value * (1.0 - gate)
        put(k, value)

    def first_left(k):
        norm_in(k)
        gated(k, k, 0, gate_a, q_a)

    def first_right(k):
        gated(k, k, 256, gate_b, q_b)

    def second_right(k):
        norm_in(8 + k)
        gated(8 + k, k, 256, gate_b, q_b)

    def second_left(k):
        gated(8 + k, k, 0, gate_a, q_a)

    fetch("pair0")
    each(0, 8, first_left)
    flush(2 * LEFT)
    pl.semaphore_wait(barrier, n_ax - 1 + n_dp - 1)
    start(2 * LEFT)
    each(0, 8, first_right)
    flush(2 * RIGHT)
    start(2 * RIGHT)
    fetch("pair1")
    each(0, 8, second_right)
    flush(2 * RIGHT + 1)
    start(2 * RIGHT + 1)
    each(0, 8, second_left)
    flush(2 * LEFT + 1)
    start(2 * LEFT + 1)

    fetch("w_out")
    fetch("gain_x")
    fetch("cot")
    wo_t[...] = w_out[...].astype(F32).T.astype(BF16)
    gx[...] = jnp.broadcast_to(jnp.broadcast_to(gain_x[...], (128, 128)).T[:, :1], (128, 256))

    def gate_row(i):
        gate = sigmoid(dot(w_t[512:640], normed[i]))
        upstream = cot[i].astype(F32).T
        lift = upstream * gate
        gate_o[i] = gate
        c_g[i] = lift * (1.0 - gate)
        lift = lift.astype(BF16)
        glift[i] = lift
        s_x[i] = dot(w_out[...], lift) * gx[...]
    each(0, 16, gate_row)
    dw[...] = jnp.zeros_like(dw)

    wait_recv(2 * LEFT)
    wait_recv(2 * RIGHT)
    wait_recv(2 * RIGHT + 1)
    for h in range(2):
        if h == 1:
            wait_recv(2 * LEFT + 1)

        def product_pair(cp):
            lefts = load_pair(2 * LEFT + h, cp)
            if h == 0:
                right0, right1 = load_pair(2 * RIGHT, cp), load_pair(2 * RIGHT + 1, cp)
            prods = []
            for e in range(2):
                left = lefts[e].reshape(128, 256).astype(BF16)
                lc[2 * cp + e, 128 * h:128 * (h + 1)] = left
                if h == 0:
                    right = jnp.concatenate([right0[e], right1[e]], axis=1).reshape(256, 256).astype(BF16)
                    rc[2 * cp + e] = right
                else:
                    right = rc[2 * cp + e]
                prods.append(dot_nt(left, right).reshape(16, 8, 256))
            store_pair(2 * PROD + h, cp, prods[0], prods[1])
        each(0, 4, product_pair)
        start(2 * PROD + h)

    for h in range(2):
        wait_recv(2 * PROD + h)
        unpack(2 * PROD + h)

        def norm_row(k):
            i = 8 * h + k
            unit, inv = stats(take(k))
            xnorm[i] = (unit * gx[...]).astype(BF16)
            scaled = s_x[i]
            mean_one = jnp.mean(scaled, axis=0, keepdims=True)
            mean_two = jnp.mean(scaled * unit, axis=0, keepdims=True)
            put(k, (scaled - mean_one - unit * mean_two) * inv)
        each(0, 8, norm_row)
        flush(2 * GPROD + h)
        start(2 * GPROD + h)

    def lift_row(i):
        flat = xnorm[i]
        lifted = dot(wo_t[...], flat)
        upd[i] = (gate_o[i] * lifted).T.astype(BF16)
        ggate = (lifted * c_g[i]).astype(BF16)
        dw[0] += dot_nt(flat, glift[i])
        dw[1] += dot_nt(normed[i], ggate)
        gnorm[i] = dot(w_in[:, 512:640], ggate)

    for h in range(2):
        wait_recv(2 * GPROD + h)

        def gleft_pair(cp):
            grads = load_pair(2 * GPROD + h, cp)
            outs = []
            for e in range(2):
                grad = grads[e].reshape(128, 256).astype(BF16)
                gc[2 * cp + e, 128 * h:128 * (h + 1)] = grad
                outs.append(dot(grad, rc[2 * cp + e]).reshape(16, 8, 256))
            store_pair(2 * GLEFT + h, cp, outs[0], outs[1])
        each(0, 4, gleft_pair)
        start(2 * GLEFT + h)
        each(8 * h, 8 * h + 8, lift_row)

    x_start(0)

    def gright_pair(cp):
        outs = [dot_tn(gc[2 * cp + e], lc[2 * cp + e]).reshape(16, 2, 8, 256) for e in range(2)]
        for h in range(2):
            store_pair(2 * GRIGHT + h, cp, outs[0][:, h], outs[1][:, h])
    each(0, 4, gright_pair)
    start(2 * GRIGHT)
    start(2 * GRIGHT + 1)
    put_out("upd")

    def back_a(h):
        def grad_row(k):
            i = 8 * h + k
            grad = take(k)
            both = jnp.concatenate([grad * gate_a[i], grad * q_a[i]], axis=0).astype(BF16)
            local = dot_nt(normed[i], both)
            dw[2] += local[:, :128]
            dw[3] += local[:, 128:]
            gnorm[i] += dot(w_in[:, 0:256], both)
        wait_recv(2 * GLEFT + h)
        unpack(2 * GLEFT + h)
        each(0, 8, grad_row)

    def back_b(h):
        wait_recv(2 * GRIGHT + h)
        unpack(2 * GRIGHT + h)
        total = jnp.concatenate([dw[4], dw[5]], axis=1)
        for k in range(8):
            i = 8 * h + k
            grad = take(k)
            both = jnp.concatenate([grad * gate_b[i], grad * q_b[i]], axis=0).astype(BF16)
            gproj[k] = both
            total += dot_nt(normed[i], both)
        dw[4] = total[:, :128]
        dw[5] = total[:, 128:]

    def out_rows(h):
        def out_row(k):
            i = 8 * h + k
            unit = unit_in[i]
            scaled = (gnorm[i] + dot(w_in[:, 256:512], gproj[k])) * gin[...]
            mean_one = jnp.mean(scaled, axis=0, keepdims=True)
            mean_two = jnp.mean(scaled * unit, axis=0, keepdims=True)
            gpair[i] = ((scaled - mean_one - unit * mean_two) * inv_in[i]).T.astype(BF16)
        each(0, 8, out_row)
        put_out("gpair%d" % h)

    back_a(0)
    back_a(1)
    x_start(1)
    back_b(0)
    left_axial()
    out_rows(0)
    back_b(1)
    right_start()
    left_y()
    out_rows(1)
    left_back()
    right_dp()
    left_x()
    right_back()
    for t in range(12):
        wait_send(t)
    for name in put_names:
        out_copy(name).wait()
    reduce_end()


def hand_on(
    upd_h, gpair_h, fin_h, w_in_h, w_out_h, gain_in_h, gain_x_h,
    upd_o, gpair_o, gw_in_o, gw_out_o, ggi_o, ggx_o,
    upd, gpair, gw_in, gw_out, ggi, ggx, fin, w_in, w_out, gain_in, gain_x, isem, osem,
):
    def moves(pairs, sems, first):
        return [pltpu.make_async_copy(a, b, sems.at[first + n]) for n, (a, b) in enumerate(pairs)]

    small_in = moves(((fin_h, fin), (w_in_h, w_in), (w_out_h, w_out), (gain_in_h, gain_in),
                      (gain_x_h, gain_x)), isem, 0)
    halves = pl.ds(0, 8), pl.ds(8, 8)
    big_in = moves([(a.at[h], b.at[h]) for a, b in ((upd_h, upd), (gpair_h, gpair)) for h in halves], isem, 5)
    big_out = moves([(a.at[h], b.at[h]) for a, b in ((upd, upd_o), (gpair, gpair_o)) for h in halves], osem, 0)
    small_out = moves(((gw_in, gw_in_o), (gw_out, gw_out_o), (ggi, ggi_o), (ggx, ggx_o)), osem, 4)
    for copy in small_in + big_in:
        copy.start()
    for copy in small_in:
        copy.wait()
    gw_out[...] = fin[0]
    gw_in[:, 512:640] = fin[1]
    for n in range(4):
        gw_in[:, 128 * n:128 * (n + 1)] = fin[2 + n]
    small_out[0].start()
    small_out[1].start()
    for n in range(4):
        big_in[n].wait()
        big_out[n].start()
    row_x = jnp.sum(gw_out[...] * w_out[...].astype(F32), axis=1, keepdims=True)
    ggx[...] = jnp.broadcast_to(row_x, (128, 128)).T[:1] / gain_x[...]
    row_in = jnp.sum(gw_in[...] * w_in[...].astype(F32), axis=1, keepdims=True)
    ggi[...] = jnp.broadcast_to(row_in, (128, 128)).T[:1] / gain_in[...]
    small_out[2].start()
    small_out[3].start()
    for copy in big_out + small_out:
        copy.wait()


def local(n_dp, n_ax, pair, cotangent, in_weight, out_weight, gain_in, gain_x):
    rows, width, chan = pair.shape[1:]
    factor = 1.0 / (n_dp * width * width) ** 0.5
    anywhere = pl.BlockSpec(memory_space=pl.ANY)
    cells = (rows, chan, width)
    args = (pair[0], cotangent[0], in_weight, out_weight, gain_in[None], gain_x[None])
    out_shape = (
        jax.ShapeDtypeStruct((rows, width, chan), BF16),
        jax.ShapeDtypeStruct((rows, width, chan), BF16),
        jax.ShapeDtypeStruct((128, 640), F32),
        jax.ShapeDtypeStruct((128, 128), F32),
        jax.ShapeDtypeStruct((1, 128), F32),
        jax.ShapeDtypeStruct((1, 128), F32),
    )
    sums_shape = jax.ShapeDtypeStruct((6, 128, 128), F32)
    upd, gpair, sums = pl.pallas_call(
        functools.partial(kernel, n_dp, n_ax, factor),
        name="triangle",
        out_shape=out_shape[:2] + (sums_shape,),
        in_specs=[anywhere] * 6,
        out_specs=(anywhere,) * 3,
        scratch_shapes=[pltpu.VMEM(v.shape, v.dtype) for v in args + out_shape[:2]] + [
            pltpu.SemaphoreType.DMA((7,)),
            pltpu.SemaphoreType.DMA((3,)),
            pltpu.SemaphoreType.DMA((2,)),
            pltpu.VMEM((8, 256, 256), BF16),
            pltpu.VMEM((12, 16, 64, 256), BF16),
            pltpu.VMEM((12, 16, 64, 256), BF16),
            pltpu.VMEM((2, 1024, 128), F32),
            pltpu.VMEM((2, 1024, 128), F32),
            pltpu.VMEM((8, 256, 256), BF16),
            pltpu.VMEM((8, 256, 256), BF16),
            pltpu.VMEM((8, 256, 256), BF16),
            pltpu.VMEM(cells, BF16),
            pltpu.VMEM(cells, F32),
            pltpu.VMEM((rows, 1, width), F32),
            pltpu.VMEM(cells, F32),
            pltpu.VMEM(cells, F32),
            pltpu.VMEM(cells, F32),
            pltpu.VMEM(cells, F32),
            pltpu.VMEM(cells, F32),
            pltpu.VMEM(cells, F32),
            pltpu.VMEM(cells, F32),
            pltpu.VMEM(cells, BF16),
            pltpu.VMEM(cells, BF16),
            pltpu.VMEM(cells, F32),
            pltpu.VMEM((640, 128), BF16),
            pltpu.VMEM((128, 128), BF16),
            pltpu.VMEM((128, 256), F32),
            pltpu.VMEM((128, 256), F32),
            pltpu.VMEM((6, 128, 128), F32),
            pltpu.VMEM((16, 2, 8, 128), F32),
            pltpu.VMEM((8, 2, 8, 128), F32),
            pltpu.VMEM((2, 8, 128), F32),
            pltpu.VMEM((2, 8, 128), F32),
            pltpu.VMEM((2, 4, 2, 32, 128), F32),
            pltpu.VMEM((4, 32, 128), F32),
            pltpu.VMEM((16, 8, 128), F32),
            pltpu.VMEM((2, 8, 128), F32),
            pltpu.VMEM((8, 128), F32),
            pltpu.VMEM((8, 128), F32),
            pltpu.VMEM((4, 32, 128), F32),
            pltpu.SemaphoreType.DMA((12,)),
            pltpu.SemaphoreType.DMA((12,)),
            pltpu.SemaphoreType.DMA((12,)),
            pltpu.SemaphoreType.DMA((9,)),
            pltpu.SemaphoreType.DMA((9,)),
        ],
        compiler_params=pltpu.CompilerParams(
            collective_id=0, has_side_effects=True, vmem_limit_bytes=60 * 2**20),
        cost_estimate=pl.CostEstimate(
            flops=3_300_000_000, bytes_accessed=5_000_000, transcendentals=1_600_000),
    )(*args)
    upd, gpair, gw_in, gw_out, ggi, ggx = pl.pallas_call(
        hand_on,
        name="hand_on",
        out_shape=out_shape,
        in_specs=[anywhere] * 7,
        out_specs=(anywhere,) * 6,
        scratch_shapes=[pltpu.VMEM(v.shape, v.dtype) for v in out_shape] + [
            pltpu.VMEM((6, 128, 128), F32)] + [pltpu.VMEM(v.shape, v.dtype) for v in args[2:]] + [
            pltpu.SemaphoreType.DMA((9,)),
            pltpu.SemaphoreType.DMA((8,)),
        ],
        compiler_params=pltpu.CompilerParams(vmem_limit_bytes=60 * 2**20),
    )(upd, gpair, sums, *args[2:])
    return upd[None], gpair[None], gw_in, gw_out, ggi[0], ggx[0]


def solution(mesh):
    cells = P("dp", "axial", None, None)
    n_dp, n_ax = mesh.shape["dp"], mesh.shape["axial"]
    return jax.shard_map(
        functools.partial(local, n_dp, n_ax), mesh=mesh,
        in_specs=(cells, cells, P(), P(), P(), P()),
        out_specs=(cells, cells, P(), P(), P(), P()), check_vma=False)
```

```python
import functools

import jax
import jax.numpy as jnp
from jax import lax
from jax.experimental import pallas as pl
from jax.experimental.pallas import tpu as pltpu
from jax.sharding import PartitionSpec as P

MESH = pl.DeviceIdType.MESH
F32 = jnp.float32
BF16 = jnp.bfloat16
UNROLL = 2
LEFT, RIGHT, PROD, GPROD, GLEFT, GRIGHT = range(6)


def dot(a, b):
    return lax.dot_general(a, b, (((1,), (0,)), ((), ())), preferred_element_type=F32)


def dot_nt(a, b):
    return lax.dot_general(a, b, (((1,), (1,)), ((), ())), preferred_element_type=F32)


def dot_tn(a, b):
    return lax.dot_general(a, b, (((0,), (0,)), ((), ())), preferred_element_type=F32)


def sigmoid(v):
    return 0.5 * jnp.tanh(0.5 * v) + 0.5


def stats(v):
    center = jnp.mean(v, axis=0, keepdims=True)
    shifted = v - center
    inv = lax.rsqrt(jnp.mean(shifted * shifted, axis=0, keepdims=True) + 1e-05)
    return shifted * inv, inv


def kernel(
    n_dp, n_ax, factor,
    pair_h, cot_h, w_in_h, w_out_h, gain_in_h, gain_x_h,
    upd_h, gpair_h, fin,
    pair, cot, w_in, w_out, gain_in, gain_x,
    upd, gpair, isem, osem, fsem, gproj,
    send, recv, tbuf, tbuf2, lc, rc, gc,
    normed, unit_in, inv_in, gate_a, q_a, gate_b, q_b, gate_o, s_x, c_g, glift, xnorm, gnorm,
    w_t, wo_t, gin, gx, dw, r1, r2, s1, s2, x1, xs, a1, a2, s3, s4, xg,
    ssem, rsem, lsem, asend, arecv,
):
    me = lax.axis_index("axial")
    dp = lax.axis_index("dp")
    my_z, my_y, my_c = me // 4, (me // 2) % 2, me % 2

    def peer(o):
        return ((my_z + o // 4) % 4) * 4 + ((my_y + (o // 2) % 2) % 2) * 2 + (my_c + o % 2) % 2

    def dp_peer(o):
        return (dp + o) % n_dp

    def each(lo, hi, fn, unroll=UNROLL):
        def body(i, carry):
            fn(i)
            return carry
        lax.fori_loop(lo, hi, body, 0, unroll=unroll)

    barrier = pltpu.get_barrier_semaphore()
    each(1, n_ax, lambda o: pl.semaphore_signal(
        barrier, inc=1, device_id=(dp, peer(o)), device_id_type=MESH))
    each(1, n_dp, lambda o: pl.semaphore_signal(
        barrier, inc=1, device_id=(dp_peer(o), me), device_id_type=MESH))

    half = pl.ds(0, 8), pl.ds(8, 8)
    in_pairs = {
        "w_in": (w_in_h, w_in), "gain_in": (gain_in_h, gain_in),
        "pair0": (pair_h.at[half[0]], pair.at[half[0]]), "pair1": (pair_h.at[half[1]], pair.at[half[1]]),
        "w_out": (w_out_h, w_out), "gain_x": (gain_x_h, gain_x), "cot": (cot_h, cot),
    }
    out_pairs = {
        "upd": (upd, upd_h),
        "gpair0": (gpair.at[half[0]], gpair_h.at[half[0]]), "gpair1": (gpair.at[half[1]], gpair_h.at[half[1]]),
    }
    in_names, put_names = list(in_pairs), list(out_pairs)

    def in_copy(name):
        return pltpu.make_async_copy(*in_pairs[name], isem.at[in_names.index(name)])

    def out_copy(name):
        return pltpu.make_async_copy(*out_pairs[name], osem.at[put_names.index(name)])

    def fetch(name):
        in_copy(name).wait()

    def put_out(name):
        out_copy(name).start()

    for name in in_names:
        in_copy(name).start()

    def start(t):
        def one(o):
            d = peer(o)
            pltpu.make_async_remote_copy(
                src_ref=send.at[t, d, part], dst_ref=recv.at[t, me, part],
                send_sem=ssem.at[t], recv_sem=rsem.at[t],
                device_id=(dp, d), device_id_type=MESH).start()
        for q in range(2):
            part = pl.ds(32 * q, 32)
            each(1, n_ax, one)
        pltpu.make_async_copy(send.at[t, me], recv.at[t, me], lsem.at[t]).start()

    last = 2 * GRIGHT + 1

    def lanes(n):
        return slice(128 * n, 128 * (n + 1))

    def last_copy(n):
        return pltpu.make_async_copy(
            send.at[last, me, :, lanes(n)], recv.at[last, me, :, lanes(n)], lsem.at[last + n])

    def start_last(n):
        def one(o):
            d = peer(o)
            pltpu.make_async_remote_copy(
                src_ref=send.at[last, d, :, lanes(n)], dst_ref=recv.at[last, me, :, lanes(n)],
                send_sem=ssem.at[last + n], recv_sem=rsem.at[last + n],
                device_id=(dp, d), device_id_type=MESH).start()
        each(1, n_ax, one)
        last_copy(n).start()

    def wait_last(n):
        last_copy(n).wait()
        part = recv.at[last, pl.ds(0, n_ax - 1), :, lanes(n)]
        pltpu.make_async_copy(part, part, rsem.at[last + n]).wait()

    def wait_last_sent(n):
        part = send.at[last, pl.ds(0, n_ax - 1), :, lanes(n)]
        pltpu.make_async_copy(part, part, ssem.at[last + n]).wait()

    def wait_recv(t):
        pltpu.make_async_copy(send.at[t, me], recv.at[t, me], lsem.at[t]).wait()
        part = recv.at[t, pl.ds(0, n_ax - 1)]
        pltpu.make_async_copy(part, part, rsem.at[t]).wait()

    def wait_send(t):
        part = send.at[t, pl.ds(0, n_ax - 1)]
        pltpu.make_async_copy(part, part, ssem.at[t]).wait()

    def bytes_of(ref, sem):
        pltpu.make_async_copy(ref, ref, sem).wait()

    def push(src, dst, k, dp_index, ax_index):
        pltpu.make_async_remote_copy(
            src_ref=src, dst_ref=dst, send_sem=asend.at[k], recv_sem=arecv.at[k],
            device_id=(dp_index, ax_index), device_id_type=MESH).start()

    def rows8(n):
        return pl.ds(pl.multiple_of(8 * n, 8), 8)

    def rows32(n):
        return pl.ds(pl.multiple_of(32 * n, 32), 32)

    right_blocks = pl.ds(4, 2)
    others = pl.ds(0, n_ax - 1)

    def right_start():
        def one(o):
            d = peer(o)
            push(dw.at[right_blocks, rows8(d)], r1.at[me], 0, dp, d)
        each(1, n_ax, one)
        r1[me] = dw[4:6, rows8(me)]

    def right_dp():
        bytes_of(r1.at[others], arecv.at[0])
        total = jnp.sum(r1[...], axis=0)
        s1[...] = total
        r2[dp] = total
        each(1, n_dp, lambda o: push(s1, r2.at[dp], 1, dp_peer(o), me))

    def right_back():
        bytes_of(r2.at[pl.ds(0, n_dp - 1)], arecv.at[1])
        s2[...] = jnp.sum(r2[...], axis=0) * factor
        target = fin.at[right_blocks, rows8(me)]
        pltpu.make_async_copy(s2, target, fsem.at[0]).start()
        each(1, n_ax, lambda o: push(s2, target, 2, dp, peer(o)))

    my_x, my_yl = dp % 4, dp // 4

    def x_peer(o):
        return my_yl * 4 + (my_x + o) % 4

    def x_start(p):
        def one(o):
            push(dw.at[pl.ds(2 * p, 2), rows32((my_x + o) % 4)], x1.at[p, my_x], 3 + p, x_peer(o), me)
        each(1, 4, one)
        x1[p, my_x] = dw[2 * p:2 * p + 2, rows32(my_x)]

    def left_axial():
        for p in range(2):
            bytes_of(x1.at[p, pl.ds(0, 3)], arecv.at[3 + p])
            xs[2 * p:2 * p + 2] = jnp.sum(x1[p], axis=0)

        def one(o):
            d = peer(o)
            push(xs.at[d // 4, rows8(d % 4)], a1.at[me], 5, dp, d)
        each(1, n_ax, one)
        a1[me] = xs[me // 4, rows8(me % 4)]

    def left_y():
        bytes_of(a1.at[others], arecv.at[5])
        total = jnp.sum(a1[...], axis=0)
        s3[...] = total
        a2[my_yl] = total
        push(s3, a2.at[my_yl], 6, (dp + 4) % 8, me)

    def left_back():
        bytes_of(a2.at[0], arecv.at[6])
        total = (a2[0] + a2[1]) * factor
        s4[...] = total
        xg[me // 4, rows8(me % 4)] = total
        each(1, n_ax, lambda o: push(s4, xg.at[me // 4, rows8(me % 4)], 7, dp, peer(o)))

    def left_x():
        bytes_of(a1.at[others], arecv.at[7])
        target = fin.at[pl.ds(0, 4), rows32(my_x)]
        pltpu.make_async_copy(xg, target, fsem.at[1]).start()
        each(1, 4, lambda o: push(xg, target, 8, x_peer(o), me))

    def reduce_end():
        for sem in (asend, arecv):
            bytes_of(fin.at[right_blocks, pl.ds(0, 8 * (n_ax - 1))], sem.at[2])
            bytes_of(fin.at[pl.ds(0, 4), pl.ds(0, 96)], sem.at[8])
        bytes_of(r1.at[others], asend.at[0])
        bytes_of(r2.at[pl.ds(0, n_dp - 1)], asend.at[1])
        for p in range(2):
            bytes_of(x1.at[p, pl.ds(0, 3)], asend.at[3 + p])
        bytes_of(a1.at[others], asend.at[5])
        bytes_of(a2.at[0], asend.at[6])
        bytes_of(a1.at[others], asend.at[7])
        pltpu.make_async_copy(s2, fin.at[right_blocks, rows8(me)], fsem.at[0]).wait()
        pltpu.make_async_copy(xg, fin.at[pl.ds(0, 4), rows32(my_x)], fsem.at[1]).wait()

    def strided(i):
        return pl.ds(i, 128, stride=8)

    def put(k, values):
        tbuf2[0, strided(k), :] = values[:, :128]
        tbuf2[1, strided(k), :] = values[:, 128:]

    def take(k):
        return jnp.concatenate([tbuf[0, strided(k), :], tbuf[1, strided(k), :]], axis=1)

    def flush(t):
        for n in range(2):
            send[t, :, :, 128 * n:128 * (n + 1)] = tbuf2[n].astype(BF16).reshape(16, 64, 128)

    def unpack(t):
        for n in range(2):
            tbuf[n] = recv[t, :, :, 128 * n:128 * (n + 1)].astype(F32).reshape(1024, 128)

    def load_pair(t, cp):
        both = recv[t, :, pl.ds(pl.multiple_of(16 * cp, 16), 16), :].astype(F32).reshape(16, 2, 8, 256)
        return both[:, 0], both[:, 1]

    def store_pair(t, cp, even, odd):
        both = jnp.concatenate([even, odd], axis=1).astype(BF16)
        send[t, :, pl.ds(pl.multiple_of(16 * cp, 16), 16), :] = both

    fetch("w_in")
    w_t[...] = w_in[...].astype(F32).T.astype(BF16)
    fetch("gain_in")
    gin[...] = jnp.broadcast_to(jnp.broadcast_to(gain_in[...], (128, 128)).T[:, :1], (128, 256))

    def norm_in(i):
        unit, inv = stats(pair[i].astype(F32).T)
        unit_in[i] = unit
        inv_in[i] = inv
        normed[i] = (unit * gin[...]).astype(BF16)

    def gated(i, k, lo, gate_ref, q_ref):
        projected = dot(w_t[lo:lo + 256], normed[i])
        gate = sigmoid(projected[128:])
        value = projected[:128] * gate
        gate_ref[i] = gate
        q_ref[i] = value * (1.0 - gate)
        put(k, value)

    def first_left(k):
        norm_in(k)
        gated(k, k, 0, gate_a, q_a)

    def first_right(k):
        gated(k, k, 256, gate_b, q_b)

    def second_right(k):
        norm_in(8 + k)
        gated(8 + k, k, 256, gate_b, q_b)

    def second_left(k):
        gated(8 + k, k, 0, gate_a, q_a)

    fetch("pair0")
    each(0, 8, first_left)
    flush(2 * LEFT)
    pl.semaphore_wait(barrier, n_ax - 1 + n_dp - 1)
    start(2 * LEFT)
    each(0, 8, first_right)
    flush(2 * RIGHT)
    start(2 * RIGHT)
    fetch("pair1")
    each(0, 8, second_right)
    flush(2 * RIGHT + 1)
    start(2 * RIGHT + 1)
    each(0, 8, second_left)
    flush(2 * LEFT + 1)
    start(2 * LEFT + 1)

    fetch("w_out")
    fetch("gain_x")
    fetch("cot")
    wo_t[...] = w_out[...].astype(F32).T.astype(BF16)
    gx[...] = jnp.broadcast_to(jnp.broadcast_to(gain_x[...], (128, 128)).T[:, :1], (128, 256))

    def gate_row(i):
        gate = sigmoid(dot(w_t[512:640], normed[i]))
        upstream = cot[i].astype(F32).T
        lift = upstream * gate
        gate_o[i] = gate
        c_g[i] = lift * (1.0 - gate)
        lift = lift.astype(BF16)
        glift[i] = lift
        s_x[i] = dot(w_out[...], lift) * gx[...]
    each(0, 16, gate_row)
    dw[...] = jnp.zeros_like(dw)

    wait_recv(2 * LEFT)
    wait_recv(2 * RIGHT)
    wait_recv(2 * RIGHT + 1)
    for h in range(2):
        if h == 1:
            wait_recv(2 * LEFT + 1)

        def product_pair(cp):
            lefts = load_pair(2 * LEFT + h, cp)
            if h == 0:
                right0, right1 = load_pair(2 * RIGHT, cp), load_pair(2 * RIGHT + 1, cp)
            prods = []
            for e in range(2):
                left = lefts[e].reshape(128, 256).astype(BF16)
                lc[2 * cp + e, 128 * h:128 * (h + 1)] = left
                if h == 0:
                    right = jnp.concatenate([right0[e], right1[e]], axis=1).reshape(256, 256).astype(BF16)
                    rc[2 * cp + e] = right
                else:
                    right = rc[2 * cp + e]
                prods.append(dot_nt(left, right).reshape(16, 8, 256))
            store_pair(2 * PROD + h, cp, prods[0], prods[1])
        each(0, 4, product_pair)
        start(2 * PROD + h)

    for h in range(2):
        wait_recv(2 * PROD + h)
        unpack(2 * PROD + h)

        def norm_row(k):
            i = 8 * h + k
            unit, inv = stats(take(k))
            xnorm[i] = (unit * gx[...]).astype(BF16)
            scaled = s_x[i]
            mean_one = jnp.mean(scaled, axis=0, keepdims=True)
            mean_two = jnp.mean(scaled * unit, axis=0, keepdims=True)
            put(k, (scaled - mean_one - unit * mean_two) * inv)
        each(0, 8, norm_row)
        flush(2 * GPROD + h)
        start(2 * GPROD + h)

    def lift_row(i):
        flat = xnorm[i]
        lifted = dot(wo_t[...], flat)
        upd[i] = (gate_o[i] * lifted).T.astype(BF16)
        ggate = (lifted * c_g[i]).astype(BF16)
        dw[0] += dot_nt(flat, glift[i])
        dw[1] += dot_nt(normed[i], ggate)
        gnorm[i] = dot(w_in[:, 512:640], ggate)

    for h in range(2):
        wait_recv(2 * GPROD + h)

        def gleft_pair(cp):
            grads = load_pair(2 * GPROD + h, cp)
            outs = []
            for e in range(2):
                grad = grads[e].reshape(128, 256).astype(BF16)
                gc[2 * cp + e, 128 * h:128 * (h + 1)] = grad
                outs.append(dot(grad, rc[2 * cp + e]).reshape(16, 8, 256))
            store_pair(2 * GLEFT + h, cp, outs[0], outs[1])
        each(0, 4, gleft_pair)
        start(2 * GLEFT + h)
        each(8 * h, 8 * h + 8, lift_row)

    x_start(0)

    def gright_pair(cp):
        outs = [dot_tn(gc[2 * cp + e], lc[2 * cp + e]).reshape(16, 2, 8, 256) for e in range(2)]
        for h in range(2):
            store_pair(2 * GRIGHT + h, cp, outs[0][:, h], outs[1][:, h])
    each(0, 4, gright_pair)
    start(2 * GRIGHT)
    start_last(0)
    start_last(1)
    put_out("upd")

    def back_a(h):
        def grad_row(k):
            i = 8 * h + k
            grad = take(k)
            both = jnp.concatenate([grad * gate_a[i], grad * q_a[i]], axis=0).astype(BF16)
            local = dot_nt(normed[i], both)
            dw[2] += local[:, :128]
            dw[3] += local[:, 128:]
            gnorm[i] += dot(w_in[:, 0:256], both)
        wait_recv(2 * GLEFT + h)
        unpack(2 * GLEFT + h)
        each(0, 8, grad_row)

    def back_b(h):
        total = jnp.concatenate([dw[4], dw[5]], axis=1)
        if h == 0:
            wait_recv(2 * GRIGHT)
        for n in range(2):
            if h == 1:
                wait_last(n)
            tbuf[n] = recv[2 * GRIGHT + h, :, :, lanes(n)].astype(F32).reshape(1024, 128)
            for k in range(0, 8, 2):
                sides = []
                for e in (k, k + 1):
                    i = 8 * h + e
                    grad = tbuf[n, strided(e), :]
                    both = jnp.concatenate(
                        [grad * gate_b[i, :, lanes(n)], grad * q_b[i, :, lanes(n)]], axis=0).astype(BF16)
                    gproj[e, :, lanes(n)] = both
                    sides.append((normed[i, :, lanes(n)], both))
                total += dot_nt(
                    jnp.concatenate([sides[0][0], sides[1][0]], axis=1),
                    jnp.concatenate([sides[0][1], sides[1][1]], axis=1))
        dw[4] = total[:, :128]
        dw[5] = total[:, 128:]

    def out_rows(h):
        def out_row(k):
            i = 8 * h + k
            unit = unit_in[i]
            scaled = (gnorm[i] + dot(w_in[:, 256:512], gproj[k])) * gin[...]
            mean_one = jnp.mean(scaled, axis=0, keepdims=True)
            mean_two = jnp.mean(scaled * unit, axis=0, keepdims=True)
            gpair[i] = ((scaled - mean_one - unit * mean_two) * inv_in[i]).T.astype(BF16)
        each(0, 8, out_row)
        put_out("gpair%d" % h)

    back_a(0)
    back_a(1)
    x_start(1)
    back_b(0)
    left_axial()
    out_rows(0)
    back_b(1)
    right_start()
    left_y()
    out_rows(1)
    left_back()
    right_dp()
    left_x()
    right_back()
    for t in range(11):
        wait_send(t)
    for n in range(2):
        wait_last_sent(n)
    for name in put_names:
        out_copy(name).wait()
    reduce_end()


def hand_on(
    upd_h, gpair_h, fin_h, w_in_h, w_out_h, gain_in_h, gain_x_h,
    upd_o, gpair_o, gw_in_o, gw_out_o, ggi_o, ggx_o,
    upd, gpair, gw_in, gw_out, ggi, ggx, fin, w_in, w_out, gain_in, gain_x, isem, osem,
):
    def moves(pairs, sems, first):
        return [pltpu.make_async_copy(a, b, sems.at[first + n]) for n, (a, b) in enumerate(pairs)]

    small_in = moves(((fin_h, fin), (w_in_h, w_in), (w_out_h, w_out), (gain_in_h, gain_in),
                      (gain_x_h, gain_x)), isem, 0)
    halves = pl.ds(0, 8), pl.ds(8, 8)
    big_in = moves([(a.at[h], b.at[h]) for a, b in ((upd_h, upd), (gpair_h, gpair)) for h in halves], isem, 5)
    big_out = moves([(a.at[h], b.at[h]) for a, b in ((upd, upd_o), (gpair, gpair_o)) for h in halves], osem, 0)
    small_out = moves(((gw_in, gw_in_o), (gw_out, gw_out_o), (ggi, ggi_o), (ggx, ggx_o)), osem, 4)
    for copy in small_in + big_in:
        copy.start()
    for copy in small_in:
        copy.wait()
    gw_out[...] = fin[0]
    gw_in[:, 512:640] = fin[1]
    for n in range(4):
        gw_in[:, 128 * n:128 * (n + 1)] = fin[2 + n]
    small_out[0].start()
    small_out[1].start()
    for n in range(4):
        big_in[n].wait()
        big_out[n].start()
    row_x = jnp.sum(gw_out[...] * w_out[...].astype(F32), axis=1, keepdims=True)
    ggx[...] = jnp.broadcast_to(row_x, (128, 128)).T[:1] / gain_x[...]
    row_in = jnp.sum(gw_in[...] * w_in[...].astype(F32), axis=1, keepdims=True)
    ggi[...] = jnp.broadcast_to(row_in, (128, 128)).T[:1] / gain_in[...]
    small_out[2].start()
    small_out[3].start()
    for copy in big_out + small_out:
        copy.wait()


def local(n_dp, n_ax, pair, cotangent, in_weight, out_weight, gain_in, gain_x):
    rows, width, chan = pair.shape[1:]
    factor = 1.0 / (n_dp * width * width) ** 0.5
    anywhere = pl.BlockSpec(memory_space=pl.ANY)
    cells = (rows, chan, width)
    args = (pair[0], cotangent[0], in_weight, out_weight, gain_in[None], gain_x[None])
    out_shape = (
        jax.ShapeDtypeStruct((rows, width, chan), BF16),
        jax.ShapeDtypeStruct((rows, width, chan), BF16),
        jax.ShapeDtypeStruct((128, 640), F32),
        jax.ShapeDtypeStruct((128, 128), F32),
        jax.ShapeDtypeStruct((1, 128), F32),
        jax.ShapeDtypeStruct((1, 128), F32),
    )
    sums_shape = jax.ShapeDtypeStruct((6, 128, 128), F32)
    upd, gpair, sums = pl.pallas_call(
        functools.partial(kernel, n_dp, n_ax, factor),
        name="triangle",
        out_shape=out_shape[:2] + (sums_shape,),
        in_specs=[anywhere] * 6,
        out_specs=(anywhere,) * 3,
        scratch_shapes=[pltpu.VMEM(v.shape, v.dtype) for v in args + out_shape[:2]] + [
            pltpu.SemaphoreType.DMA((7,)),
            pltpu.SemaphoreType.DMA((3,)),
            pltpu.SemaphoreType.DMA((2,)),
            pltpu.VMEM((8, 256, 256), BF16),
            pltpu.VMEM((12, 16, 64, 256), BF16),
            pltpu.VMEM((12, 16, 64, 256), BF16),
            pltpu.VMEM((2, 1024, 128), F32),
            pltpu.VMEM((2, 1024, 128), F32),
            pltpu.VMEM((8, 256, 256), BF16),
            pltpu.VMEM((8, 256, 256), BF16),
            pltpu.VMEM((8, 256, 256), BF16),
            pltpu.VMEM(cells, BF16),
            pltpu.VMEM(cells, F32),
            pltpu.VMEM((rows, 1, width), F32),
            pltpu.VMEM(cells, F32),
            pltpu.VMEM(cells, F32),
            pltpu.VMEM(cells, F32),
            pltpu.VMEM(cells, F32),
            pltpu.VMEM(cells, F32),
            pltpu.VMEM(cells, F32),
            pltpu.VMEM(cells, F32),
            pltpu.VMEM(cells, BF16),
            pltpu.VMEM(cells, BF16),
            pltpu.VMEM(cells, F32),
            pltpu.VMEM((640, 128), BF16),
            pltpu.VMEM((128, 128), BF16),
            pltpu.VMEM((128, 256), F32),
            pltpu.VMEM((128, 256), F32),
            pltpu.VMEM((6, 128, 128), F32),
            pltpu.VMEM((16, 2, 8, 128), F32),
            pltpu.VMEM((8, 2, 8, 128), F32),
            pltpu.VMEM((2, 8, 128), F32),
            pltpu.VMEM((2, 8, 128), F32),
            pltpu.VMEM((2, 4, 2, 32, 128), F32),
            pltpu.VMEM((4, 32, 128), F32),
            pltpu.VMEM((16, 8, 128), F32),
            pltpu.VMEM((2, 8, 128), F32),
            pltpu.VMEM((8, 128), F32),
            pltpu.VMEM((8, 128), F32),
            pltpu.VMEM((4, 32, 128), F32),
            pltpu.SemaphoreType.DMA((13,)),
            pltpu.SemaphoreType.DMA((13,)),
            pltpu.SemaphoreType.DMA((13,)),
            pltpu.SemaphoreType.DMA((9,)),
            pltpu.SemaphoreType.DMA((9,)),
        ],
        compiler_params=pltpu.CompilerParams(
            collective_id=0, has_side_effects=True, vmem_limit_bytes=60 * 2**20),
        cost_estimate=pl.CostEstimate(
            flops=3_300_000_000, bytes_accessed=5_000_000, transcendentals=1_600_000),
    )(*args)
    upd, gpair, gw_in, gw_out, ggi, ggx = pl.pallas_call(
        hand_on,
        name="hand_on",
        out_shape=out_shape,
        in_specs=[anywhere] * 7,
        out_specs=(anywhere,) * 6,
        scratch_shapes=[pltpu.VMEM(v.shape, v.dtype) for v in out_shape] + [
            pltpu.VMEM((6, 128, 128), F32)] + [pltpu.VMEM(v.shape, v.dtype) for v in args[2:]] + [
            pltpu.SemaphoreType.DMA((9,)),
            pltpu.SemaphoreType.DMA((8,)),
        ],
        compiler_params=pltpu.CompilerParams(vmem_limit_bytes=60 * 2**20),
    )(upd, gpair, sums, *args[2:])
    return upd[None], gpair[None], gw_in, gw_out, ggi[0], ggx[0]


def solution(mesh):
    cells = P("dp", "axial", None, None)
    n_dp, n_ax = mesh.shape["dp"], mesh.shape["axial"]
    return jax.shard_map(
        functools.partial(local, n_dp, n_ax), mesh=mesh,
        in_specs=(cells, cells, P(), P(), P(), P()),
        out_specs=(cells, cells, P(), P(), P(), P()), check_vma=False)
```

```python
import functools

import jax
import jax.numpy as jnp
from jax import lax
from jax.experimental import pallas as pl
from jax.experimental.pallas import tpu as pltpu
from jax.sharding import PartitionSpec as P

MESH = pl.DeviceIdType.MESH
F32 = jnp.float32
BF16 = jnp.bfloat16
UNROLL = 2
LEFT, RIGHT, PROD, GPROD, GLEFT, GRIGHT = range(6)


def dot(a, b):
    return lax.dot_general(a, b, (((1,), (0,)), ((), ())), preferred_element_type=F32)


def dot_nt(a, b):
    return lax.dot_general(a, b, (((1,), (1,)), ((), ())), preferred_element_type=F32)


def dot_tn(a, b):
    return lax.dot_general(a, b, (((0,), (0,)), ((), ())), preferred_element_type=F32)


def sigmoid(v):
    return 0.5 * jnp.tanh(0.5 * v) + 0.5


def stats(v):
    center = jnp.mean(v, axis=0, keepdims=True)
    shifted = v - center
    inv = lax.rsqrt(jnp.mean(shifted * shifted, axis=0, keepdims=True) + 1e-05)
    return shifted * inv, inv


def kernel(
    n_dp, n_ax, factor,
    pair_h, cot_h, w_in_h, w_out_h, gain_in_h, gain_x_h,
    upd_h, gpair_h, fin,
    pair, cot, w_in, w_out, gain_in, gain_x,
    upd, gpair, isem, osem, fsem, gproj,
    send, recv, tbuf, tbuf2, lc, rc, gc,
    normed, unit_in, inv_in, gate_a, q_a, gate_b, q_b, gate_o, s_x, c_g, glift, xnorm, gnorm,
    w_t, wo_t, gin, gx, dw, r1, r2, s1, s2, x1, xs, a1, a2, s3, s4, xg,
    ssem, rsem, lsem, asend, arecv,
):
    me = lax.axis_index("axial")
    dp = lax.axis_index("dp")
    my_z, my_y, my_c = me // 4, (me // 2) % 2, me % 2

    def peer(o):
        return ((my_z + o // 4) % 4) * 4 + ((my_y + (o // 2) % 2) % 2) * 2 + (my_c + o % 2) % 2

    def dp_peer(o):
        return (dp + o) % n_dp

    def each(lo, hi, fn, unroll=UNROLL):
        def body(i, carry):
            fn(i)
            return carry
        lax.fori_loop(lo, hi, body, 0, unroll=unroll)

    half = pl.ds(0, 8), pl.ds(8, 8)
    in_pairs = {
        "w_in": (w_in_h, w_in), "gain_in": (gain_in_h, gain_in),
        "pair0": (pair_h.at[half[0]], pair.at[half[0]]), "pair1": (pair_h.at[half[1]], pair.at[half[1]]),
        "w_out": (w_out_h, w_out), "gain_x": (gain_x_h, gain_x), "cot": (cot_h, cot),
    }
    out_pairs = {
        "upd": (upd, upd_h),
        "gpair0": (gpair.at[half[0]], gpair_h.at[half[0]]), "gpair1": (gpair.at[half[1]], gpair_h.at[half[1]]),
    }
    in_names, put_names = list(in_pairs), list(out_pairs)

    def in_copy(name):
        return pltpu.make_async_copy(*in_pairs[name], isem.at[in_names.index(name)])

    def out_copy(name):
        return pltpu.make_async_copy(*out_pairs[name], osem.at[put_names.index(name)])

    def fetch(name):
        in_copy(name).wait()

    def put_out(name):
        out_copy(name).start()

    for name in in_names:
        in_copy(name).start()

    barrier = pltpu.get_barrier_semaphore()
    for o in (10, 11, 6, 7, 14, 15, 8, 9, 2, 3, 4, 5, 12, 13, 1):
        pl.semaphore_signal(barrier, inc=1, device_id=(dp, peer(o)), device_id_type=MESH)
    each(1, n_dp, lambda o: pl.semaphore_signal(
        barrier, inc=1, device_id=(dp_peer(o), me), device_id_type=MESH))

    def start(t):
        def one(o):
            d = peer(o)
            pltpu.make_async_remote_copy(
                src_ref=send.at[t, d, part], dst_ref=recv.at[t, me, part],
                send_sem=ssem.at[t], recv_sem=rsem.at[t],
                device_id=(dp, d), device_id_type=MESH).start()
        for q in range(2):
            part = pl.ds(32 * q, 32)
            each(1, n_ax, one)
        pltpu.make_async_copy(send.at[t, me], recv.at[t, me], lsem.at[t]).start()

    last = 2 * GRIGHT + 1

    def lanes(n):
        return slice(128 * n, 128 * (n + 1))

    def last_copy(n):
        return pltpu.make_async_copy(
            send.at[last, me, :, lanes(n)], recv.at[last, me, :, lanes(n)], lsem.at[last + n])

    def start_last(n):
        def one(o):
            d = peer(o)
            pltpu.make_async_remote_copy(
                src_ref=send.at[last, d, :, lanes(n)], dst_ref=recv.at[last, me, :, lanes(n)],
                send_sem=ssem.at[last + n], recv_sem=rsem.at[last + n],
                device_id=(dp, d), device_id_type=MESH).start()
        each(1, n_ax, one)
        last_copy(n).start()

    def wait_last(n):
        last_copy(n).wait()
        part = recv.at[last, pl.ds(0, n_ax - 1), :, lanes(n)]
        pltpu.make_async_copy(part, part, rsem.at[last + n]).wait()

    def wait_last_sent(n):
        part = send.at[last, pl.ds(0, n_ax - 1), :, lanes(n)]
        pltpu.make_async_copy(part, part, ssem.at[last + n]).wait()

    def wait_recv(t):
        pltpu.make_async_copy(send.at[t, me], recv.at[t, me], lsem.at[t]).wait()
        part = recv.at[t, pl.ds(0, n_ax - 1)]
        pltpu.make_async_copy(part, part, rsem.at[t]).wait()

    def wait_send(t):
        part = send.at[t, pl.ds(0, n_ax - 1)]
        pltpu.make_async_copy(part, part, ssem.at[t]).wait()

    def bytes_of(ref, sem):
        pltpu.make_async_copy(ref, ref, sem).wait()

    def push(src, dst, k, dp_index, ax_index):
        pltpu.make_async_remote_copy(
            src_ref=src, dst_ref=dst, send_sem=asend.at[k], recv_sem=arecv.at[k],
            device_id=(dp_index, ax_index), device_id_type=MESH).start()

    def rows8(n):
        return pl.ds(pl.multiple_of(8 * n, 8), 8)

    def rows32(n):
        return pl.ds(pl.multiple_of(32 * n, 32), 32)

    right_blocks = pl.ds(4, 2)
    others = pl.ds(0, n_ax - 1)

    def right_start():
        def one(o):
            d = peer(o)
            push(dw.at[right_blocks, rows8(d)], r1.at[me], 0, dp, d)
        each(1, n_ax, one)
        r1[me] = dw[4:6, rows8(me)]

    def right_dp():
        bytes_of(r1.at[others], arecv.at[0])
        total = jnp.sum(r1[...], axis=0)
        s1[...] = total
        r2[dp] = total
        each(1, n_dp, lambda o: push(s1, r2.at[dp], 1, dp_peer(o), me))

    def right_back():
        bytes_of(r2.at[pl.ds(0, n_dp - 1)], arecv.at[1])
        s2[...] = jnp.sum(r2[...], axis=0) * factor
        target = fin.at[right_blocks, rows8(me)]
        pltpu.make_async_copy(s2, target, fsem.at[0]).start()
        each(1, n_ax, lambda o: push(s2, target, 2, dp, peer(o)))

    my_x, my_yl = dp % 4, dp // 4

    def x_peer(o):
        return my_yl * 4 + (my_x + o) % 4

    def x_start(p):
        def one(o):
            push(dw.at[pl.ds(2 * p, 2), rows32((my_x + o) % 4)], x1.at[p, my_x], 3 + p, x_peer(o), me)
        each(1, 4, one)
        x1[p, my_x] = dw[2 * p:2 * p + 2, rows32(my_x)]

    def left_axial():
        for p in range(2):
            bytes_of(x1.at[p, pl.ds(0, 3)], arecv.at[3 + p])
            xs[2 * p:2 * p + 2] = jnp.sum(x1[p], axis=0)

        def one(o):
            d = peer(o)
            push(xs.at[d // 4, rows8(d % 4)], a1.at[me], 5, dp, d)
        each(1, n_ax, one)
        a1[me] = xs[me // 4, rows8(me % 4)]

    def left_y():
        bytes_of(a1.at[others], arecv.at[5])
        total = jnp.sum(a1[...], axis=0)
        s3[...] = total
        a2[my_yl] = total
        push(s3, a2.at[my_yl], 6, (dp + 4) % 8, me)

    def left_back():
        bytes_of(a2.at[0], arecv.at[6])
        total = (a2[0] + a2[1]) * factor
        s4[...] = total
        xg[me // 4, rows8(me % 4)] = total
        each(1, n_ax, lambda o: push(s4, xg.at[me // 4, rows8(me % 4)], 7, dp, peer(o)))

    def left_x():
        bytes_of(a1.at[others], arecv.at[7])
        target = fin.at[pl.ds(0, 4), rows32(my_x)]
        pltpu.make_async_copy(xg, target, fsem.at[1]).start()
        each(1, 4, lambda o: push(xg, target, 8, x_peer(o), me))

    def reduce_end():
        for sem in (asend, arecv):
            bytes_of(fin.at[right_blocks, pl.ds(0, 8 * (n_ax - 1))], sem.at[2])
            bytes_of(fin.at[pl.ds(0, 4), pl.ds(0, 96)], sem.at[8])
        bytes_of(r1.at[others], asend.at[0])
        bytes_of(r2.at[pl.ds(0, n_dp - 1)], asend.at[1])
        for p in range(2):
            bytes_of(x1.at[p, pl.ds(0, 3)], asend.at[3 + p])
        bytes_of(a1.at[others], asend.at[5])
        bytes_of(a2.at[0], asend.at[6])
        bytes_of(a1.at[others], asend.at[7])
        pltpu.make_async_copy(s2, fin.at[right_blocks, rows8(me)], fsem.at[0]).wait()
        pltpu.make_async_copy(xg, fin.at[pl.ds(0, 4), rows32(my_x)], fsem.at[1]).wait()

    def strided(i):
        return pl.ds(i, 128, stride=8)

    def put(k, values):
        tbuf2[0, strided(k), :] = values[:, :128]
        tbuf2[1, strided(k), :] = values[:, 128:]

    def take(k):
        return jnp.concatenate([tbuf[0, strided(k), :], tbuf[1, strided(k), :]], axis=1)

    def flush(t):
        for n in range(2):
            send[t, :, :, 128 * n:128 * (n + 1)] = tbuf2[n].astype(BF16).reshape(16, 64, 128)

    def unpack(t):
        for n in range(2):
            tbuf[n] = recv[t, :, :, 128 * n:128 * (n + 1)].astype(F32).reshape(1024, 128)

    def load_pair(t, cp):
        both = recv[t, :, pl.ds(pl.multiple_of(16 * cp, 16), 16), :].astype(F32).reshape(16, 2, 8, 256)
        return both[:, 0], both[:, 1]

    def store_pair(t, cp, even, odd):
        both = jnp.concatenate([even, odd], axis=1).astype(BF16)
        send[t, :, pl.ds(pl.multiple_of(16 * cp, 16), 16), :] = both

    fetch("w_in")
    w_t[...] = w_in[...].astype(F32).T.astype(BF16)
    fetch("gain_in")
    gin[...] = jnp.broadcast_to(jnp.broadcast_to(gain_in[...], (128, 128)).T[:, :1], (128, 256))

    def norm_in(i):
        unit, inv = stats(pair[i].astype(F32).T)
        unit_in[i] = unit
        inv_in[i] = inv
        normed[i] = (unit * gin[...]).astype(BF16)

    def gated(i, k, lo, gate_ref, q_ref):
        projected = dot(w_t[lo:lo + 256], normed[i])
        gate = sigmoid(projected[128:])
        value = projected[:128] * gate
        gate_ref[i] = gate
        q_ref[i] = value * (1.0 - gate)
        put(k, value)

    def first_left(k):
        norm_in(k)
        gated(k, k, 0, gate_a, q_a)

    def first_right(k):
        gated(k, k, 256, gate_b, q_b)

    def second_right(k):
        norm_in(8 + k)
        gated(8 + k, k, 256, gate_b, q_b)

    def second_left(k):
        gated(8 + k, k, 0, gate_a, q_a)

    fetch("pair0")
    each(0, 8, first_left)
    flush(2 * LEFT)
    pl.semaphore_wait(barrier, n_ax - 1 + n_dp - 1)
    start(2 * LEFT)
    each(0, 8, first_right)
    flush(2 * RIGHT)
    start(2 * RIGHT)
    fetch("pair1")
    each(0, 8, second_right)
    flush(2 * RIGHT + 1)
    start(2 * RIGHT + 1)
    each(0, 8, second_left)
    flush(2 * LEFT + 1)
    start(2 * LEFT + 1)

    fetch("w_out")
    fetch("gain_x")
    fetch("cot")
    wo_t[...] = w_out[...].astype(F32).T.astype(BF16)
    gx[...] = jnp.broadcast_to(jnp.broadcast_to(gain_x[...], (128, 128)).T[:, :1], (128, 256))

    def gate_row(i):
        gate = sigmoid(dot(w_t[512:640], normed[i]))
        upstream = cot[i].astype(F32).T
        lift = upstream * gate
        gate_o[i] = gate
        c_g[i] = lift * (1.0 - gate)
        lift = lift.astype(BF16)
        glift[i] = lift
        s_x[i] = dot(w_out[...], lift) * gx[...]
    each(0, 16, gate_row)
    dw[...] = jnp.zeros_like(dw)

    wait_recv(2 * LEFT)
    wait_recv(2 * RIGHT)
    wait_recv(2 * RIGHT + 1)
    for h in range(2):
        if h == 1:
            wait_recv(2 * LEFT + 1)

        def product_pair(cp):
            lefts = load_pair(2 * LEFT + h, cp)
            if h == 0:
                right0, right1 = load_pair(2 * RIGHT, cp), load_pair(2 * RIGHT + 1, cp)
            prods = []
            for e in range(2):
                left = lefts[e].reshape(128, 256).astype(BF16)
                lc[2 * cp + e, 128 * h:128 * (h + 1)] = left
                if h == 0:
                    right = jnp.concatenate([right0[e], right1[e]], axis=1).reshape(256, 256).astype(BF16)
                    rc[2 * cp + e] = right
                else:
                    right = rc[2 * cp + e]
                prods.append(dot_nt(left, right).reshape(16, 8, 256))
            store_pair(2 * PROD + h, cp, prods[0], prods[1])
        each(0, 4, product_pair)
        start(2 * PROD + h)

    for h in range(2):
        wait_recv(2 * PROD + h)
        unpack(2 * PROD + h)

        def norm_row(k):
            i = 8 * h + k
            unit, inv = stats(take(k))
            xnorm[i] = (unit * gx[...]).astype(BF16)
            scaled = s_x[i]
            mean_one = jnp.mean(scaled, axis=0, keepdims=True)
            mean_two = jnp.mean(scaled * unit, axis=0, keepdims=True)
            put(k, (scaled - mean_one - unit * mean_two) * inv)
        each(0, 8, norm_row)
        flush(2 * GPROD + h)
        start(2 * GPROD + h)

    def lift_row(i):
        flat = xnorm[i]
        lifted = dot(wo_t[...], flat)
        upd[i] = (gate_o[i] * lifted).T.astype(BF16)
        ggate = (lifted * c_g[i]).astype(BF16)
        dw[0] += dot_nt(flat, glift[i])
        dw[1] += dot_nt(normed[i], ggate)
        gnorm[i] = dot(w_in[:, 512:640], ggate)

    for h in range(2):
        wait_recv(2 * GPROD + h)

        def gleft_pair(cp):
            grads = load_pair(2 * GPROD + h, cp)
            outs = []
            for e in range(2):
                grad = grads[e].reshape(128, 256).astype(BF16)
                gc[2 * cp + e, 128 * h:128 * (h + 1)] = grad
                outs.append(dot(grad, rc[2 * cp + e]).reshape(16, 8, 256))
            store_pair(2 * GLEFT + h, cp, outs[0], outs[1])
        each(0, 4, gleft_pair)
        start(2 * GLEFT + h)
        each(8 * h, 8 * h + 8, lift_row)

    x_start(0)

    def gright_pair(cp):
        outs = [dot_tn(gc[2 * cp + e], lc[2 * cp + e]).reshape(16, 2, 8, 256) for e in range(2)]
        for h in range(2):
            store_pair(2 * GRIGHT + h, cp, outs[0][:, h], outs[1][:, h])
    each(0, 4, gright_pair)
    start(2 * GRIGHT)
    start_last(0)
    start_last(1)
    put_out("upd")

    def back_a(h):
        def grad_row(k):
            i = 8 * h + k
            grad = take(k)
            both = jnp.concatenate([grad * gate_a[i], grad * q_a[i]], axis=0).astype(BF16)
            local = dot_nt(normed[i], both)
            dw[2] += local[:, :128]
            dw[3] += local[:, 128:]
            gnorm[i] += dot(w_in[:, 0:256], both)
        wait_recv(2 * GLEFT + h)
        unpack(2 * GLEFT + h)
        each(0, 8, grad_row)

    def back_b(h):
        total = jnp.concatenate([dw[4], dw[5]], axis=1)
        if h == 0:
            wait_recv(2 * GRIGHT)
        for n in range(2):
            if h == 1:
                wait_last(n)
            tbuf[n] = recv[2 * GRIGHT + h, :, :, lanes(n)].astype(F32).reshape(1024, 128)
            for k in range(0, 8, 2):
                sides = []
                for e in (k, k + 1):
                    i = 8 * h + e
                    grad = tbuf[n, strided(e), :]
                    both = jnp.concatenate(
                        [grad * gate_b[i, :, lanes(n)], grad * q_b[i, :, lanes(n)]], axis=0).astype(BF16)
                    gproj[e, :, lanes(n)] = both
                    sides.append((normed[i, :, lanes(n)], both))
                total += dot_nt(
                    jnp.concatenate([sides[0][0], sides[1][0]], axis=1),
                    jnp.concatenate([sides[0][1], sides[1][1]], axis=1))
        dw[4] = total[:, :128]
        dw[5] = total[:, 128:]

    def out_rows(h):
        def out_row(k):
            i = 8 * h + k
            unit = unit_in[i]
            scaled = (gnorm[i] + dot(w_in[:, 256:512], gproj[k])) * gin[...]
            mean_one = jnp.mean(scaled, axis=0, keepdims=True)
            mean_two = jnp.mean(scaled * unit, axis=0, keepdims=True)
            gpair[i] = ((scaled - mean_one - unit * mean_two) * inv_in[i]).T.astype(BF16)
        each(0, 8, out_row)
        put_out("gpair%d" % h)

    back_a(0)
    back_a(1)
    x_start(1)
    back_b(0)
    left_axial()
    out_rows(0)
    back_b(1)
    right_start()
    left_y()
    out_rows(1)
    left_back()
    right_dp()
    left_x()
    right_back()
    for t in range(11):
        wait_send(t)
    for n in range(2):
        wait_last_sent(n)
    for name in put_names:
        out_copy(name).wait()
    reduce_end()


def hand_on(
    upd_h, gpair_h, fin_h, w_in_h, w_out_h, gain_in_h, gain_x_h,
    upd_o, gpair_o, gw_in_o, gw_out_o, ggi_o, ggx_o,
    upd, gpair, gw_in, gw_out, ggi, ggx, fin, w_in, w_out, gain_in, gain_x, isem, osem,
):
    def moves(pairs, sems, first):
        return [pltpu.make_async_copy(a, b, sems.at[first + n]) for n, (a, b) in enumerate(pairs)]

    small_in = moves(((fin_h, fin), (w_in_h, w_in), (w_out_h, w_out), (gain_in_h, gain_in),
                      (gain_x_h, gain_x)), isem, 0)
    halves = pl.ds(0, 8), pl.ds(8, 8)
    big_in = moves([(a.at[h], b.at[h]) for a, b in ((upd_h, upd), (gpair_h, gpair)) for h in halves], isem, 5)
    big_out = moves([(a.at[h], b.at[h]) for a, b in ((upd, upd_o), (gpair, gpair_o)) for h in halves], osem, 0)
    small_out = moves(((gw_in, gw_in_o), (gw_out, gw_out_o), (ggi, ggi_o), (ggx, ggx_o)), osem, 4)
    for copy in small_in + big_in:
        copy.start()
    for copy in small_in:
        copy.wait()
    gw_out[...] = fin[0]
    gw_in[:, 512:640] = fin[1]
    for n in range(4):
        gw_in[:, 128 * n:128 * (n + 1)] = fin[2 + n]
    small_out[0].start()
    small_out[1].start()
    for n in range(4):
        big_in[n].wait()
        big_out[n].start()
    row_x = jnp.sum(gw_out[...] * w_out[...].astype(F32), axis=1, keepdims=True)
    ggx[...] = jnp.broadcast_to(row_x, (128, 128)).T[:1] / gain_x[...]
    row_in = jnp.sum(gw_in[...] * w_in[...].astype(F32), axis=1, keepdims=True)
    ggi[...] = jnp.broadcast_to(row_in, (128, 128)).T[:1] / gain_in[...]
    small_out[2].start()
    small_out[3].start()
    for copy in big_out + small_out:
        copy.wait()


def local(n_dp, n_ax, pair, cotangent, in_weight, out_weight, gain_in, gain_x):
    rows, width, chan = pair.shape[1:]
    factor = 1.0 / (n_dp * width * width) ** 0.5
    anywhere = pl.BlockSpec(memory_space=pl.ANY)
    cells = (rows, chan, width)
    args = (pair[0], cotangent[0], in_weight, out_weight, gain_in[None], gain_x[None])
    out_shape = (
        jax.ShapeDtypeStruct((rows, width, chan), BF16),
        jax.ShapeDtypeStruct((rows, width, chan), BF16),
        jax.ShapeDtypeStruct((128, 640), F32),
        jax.ShapeDtypeStruct((128, 128), F32),
        jax.ShapeDtypeStruct((1, 128), F32),
        jax.ShapeDtypeStruct((1, 128), F32),
    )
    sums_shape = jax.ShapeDtypeStruct((6, 128, 128), F32)
    upd, gpair, sums = pl.pallas_call(
        functools.partial(kernel, n_dp, n_ax, factor),
        name="triangle",
        out_shape=out_shape[:2] + (sums_shape,),
        in_specs=[anywhere] * 6,
        out_specs=(anywhere,) * 3,
        scratch_shapes=[pltpu.VMEM(v.shape, v.dtype) for v in args + out_shape[:2]] + [
            pltpu.SemaphoreType.DMA((7,)),
            pltpu.SemaphoreType.DMA((3,)),
            pltpu.SemaphoreType.DMA((2,)),
            pltpu.VMEM((8, 256, 256), BF16),
            pltpu.VMEM((12, 16, 64, 256), BF16),
            pltpu.VMEM((12, 16, 64, 256), BF16),
            pltpu.VMEM((2, 1024, 128), F32),
            pltpu.VMEM((2, 1024, 128), F32),
            pltpu.VMEM((8, 256, 256), BF16),
            pltpu.VMEM((8, 256, 256), BF16),
            pltpu.VMEM((8, 256, 256), BF16),
            pltpu.VMEM(cells, BF16),
            pltpu.VMEM(cells, F32),
            pltpu.VMEM((rows, 1, width), F32),
            pltpu.VMEM(cells, F32),
            pltpu.VMEM(cells, F32),
            pltpu.VMEM(cells, F32),
            pltpu.VMEM(cells, F32),
            pltpu.VMEM(cells, F32),
            pltpu.VMEM(cells, F32),
            pltpu.VMEM(cells, F32),
            pltpu.VMEM(cells, BF16),
            pltpu.VMEM(cells, BF16),
            pltpu.VMEM(cells, F32),
            pltpu.VMEM((640, 128), BF16),
            pltpu.VMEM((128, 128), BF16),
            pltpu.VMEM((128, 256), F32),
            pltpu.VMEM((128, 256), F32),
            pltpu.VMEM((6, 128, 128), F32),
            pltpu.VMEM((16, 2, 8, 128), F32),
            pltpu.VMEM((8, 2, 8, 128), F32),
            pltpu.VMEM((2, 8, 128), F32),
            pltpu.VMEM((2, 8, 128), F32),
            pltpu.VMEM((2, 4, 2, 32, 128), F32),
            pltpu.VMEM((4, 32, 128), F32),
            pltpu.VMEM((16, 8, 128), F32),
            pltpu.VMEM((2, 8, 128), F32),
            pltpu.VMEM((8, 128), F32),
            pltpu.VMEM((8, 128), F32),
            pltpu.VMEM((4, 32, 128), F32),
            pltpu.SemaphoreType.DMA((13,)),
            pltpu.SemaphoreType.DMA((13,)),
            pltpu.SemaphoreType.DMA((13,)),
            pltpu.SemaphoreType.DMA((9,)),
            pltpu.SemaphoreType.DMA((9,)),
        ],
        compiler_params=pltpu.CompilerParams(
            collective_id=0, has_side_effects=True, vmem_limit_bytes=60 * 2**20),
        cost_estimate=pl.CostEstimate(
            flops=3_300_000_000, bytes_accessed=5_000_000, transcendentals=1_600_000),
    )(*args)
    upd, gpair, gw_in, gw_out, ggi, ggx = pl.pallas_call(
        hand_on,
        name="hand_on",
        out_shape=out_shape,
        in_specs=[anywhere] * 7,
        out_specs=(anywhere,) * 6,
        scratch_shapes=[pltpu.VMEM(v.shape, v.dtype) for v in out_shape] + [
            pltpu.VMEM((6, 128, 128), F32)] + [pltpu.VMEM(v.shape, v.dtype) for v in args[2:]] + [
            pltpu.SemaphoreType.DMA((9,)),
            pltpu.SemaphoreType.DMA((8,)),
        ],
        compiler_params=pltpu.CompilerParams(vmem_limit_bytes=60 * 2**20),
    )(upd, gpair, sums, *args[2:])
    return upd[None], gpair[None], gw_in, gw_out, ggi[0], ggx[0]


def solution(mesh):
    cells = P("dp", "axial", None, None)
    n_dp, n_ax = mesh.shape["dp"], mesh.shape["axial"]
    return jax.shard_map(
        functools.partial(local, n_dp, n_ax), mesh=mesh,
        in_specs=(cells, cells, P(), P(), P(), P()),
        out_specs=(cells, cells, P(), P(), P(), P()), check_vma=False)
```

```python
import functools

import jax
import jax.numpy as jnp
from jax import lax
from jax.experimental import pallas as pl
from jax.experimental.pallas import tpu as pltpu
from jax.sharding import PartitionSpec as P

MESH = pl.DeviceIdType.MESH
F32 = jnp.float32
BF16 = jnp.bfloat16
UNROLL = 2
LEFT, RIGHT, PROD, GPROD, GLEFT, GRIGHT = range(6)


def dot(a, b):
    return lax.dot_general(a, b, (((1,), (0,)), ((), ())), preferred_element_type=F32)


def dot_nt(a, b):
    return lax.dot_general(a, b, (((1,), (1,)), ((), ())), preferred_element_type=F32)


def dot_tn(a, b):
    return lax.dot_general(a, b, (((0,), (0,)), ((), ())), preferred_element_type=F32)


def sigmoid(v):
    return 0.5 * jnp.tanh(0.5 * v) + 0.5


def stats(v):
    center = jnp.mean(v, axis=0, keepdims=True)
    shifted = v - center
    inv = lax.rsqrt(jnp.mean(shifted * shifted, axis=0, keepdims=True) + 1e-05)
    return shifted * inv, inv


def kernel(
    n_dp, n_ax, factor,
    pair_h, cot_h, w_in_h, w_out_h, gain_in_h, gain_x_h,
    upd_h, gpair_h, fin,
    pair, cot, w_in, w_out, gain_in, gain_x,
    upd, gpair, isem, osem, fsem, gproj,
    send, recv, tbuf, tbuf2, lc, rc, gc,
    normed, unit_in, inv_in, gate_a, q_a, gate_b, q_b, gate_o, s_x, c_g, glift, xnorm, gnorm,
    w_t, wo_t, gin, gx, dw, r1, r2, s1, s2, x1, xs, a1, a2, s3, s4, xg,
    ssem, rsem, lsem, asend, arecv,
):
    me = lax.axis_index("axial")
    dp = lax.axis_index("dp")
    my_z, my_y, my_c = me // 4, (me // 2) % 2, me % 2
    far_first = (10, 11, 6, 7, 14, 15, 8, 9, 2, 3, 4, 5, 12, 13, 1)

    def peer(o):
        return ((my_z + o // 4) % 4) * 4 + ((my_y + (o // 2) % 2) % 2) * 2 + (my_c + o % 2) % 2

    def dp_peer(o):
        return (dp + o) % n_dp

    def each(lo, hi, fn, unroll=UNROLL):
        def body(i, carry):
            fn(i)
            return carry
        lax.fori_loop(lo, hi, body, 0, unroll=unroll)

    half = pl.ds(0, 8), pl.ds(8, 8)
    in_pairs = {
        "w_in": (w_in_h, w_in), "gain_in": (gain_in_h, gain_in),
        "pair0": (pair_h.at[half[0]], pair.at[half[0]]), "pair1": (pair_h.at[half[1]], pair.at[half[1]]),
        "w_out": (w_out_h, w_out), "gain_x": (gain_x_h, gain_x), "cot": (cot_h, cot),
    }
    out_pairs = {
        "upd": (upd, upd_h),
        "gpair0": (gpair.at[half[0]], gpair_h.at[half[0]]), "gpair1": (gpair.at[half[1]], gpair_h.at[half[1]]),
    }
    in_names, put_names = list(in_pairs), list(out_pairs)

    def in_copy(name):
        return pltpu.make_async_copy(*in_pairs[name], isem.at[in_names.index(name)])

    def out_copy(name):
        return pltpu.make_async_copy(*out_pairs[name], osem.at[put_names.index(name)])

    def fetch(name):
        in_copy(name).wait()

    def put_out(name):
        out_copy(name).start()

    for name in in_names:
        in_copy(name).start()

    barrier = pltpu.get_barrier_semaphore()

    def greet(dp_index, ax_index):
        pl.semaphore_signal(barrier, inc=1, device_id=(dp_index, ax_index), device_id_type=MESH)

    def greet_dp(o):
        greet((dp // 4 + o // 4) % 2 * 4 + (dp % 4 + o % 4) % 4, me)

    for o in far_first[:6]:
        greet(dp, peer(o))
    for o in (6, 5, 7, 2):
        greet_dp(o)
    for o in far_first[6:14]:
        greet(dp, peer(o))
    for o in (1, 3, 4):
        greet_dp(o)
    greet(dp, peer(1))

    def start(t):
        def one(o):
            d = peer(o)
            pltpu.make_async_remote_copy(
                src_ref=send.at[t, d, part], dst_ref=recv.at[t, me, part],
                send_sem=ssem.at[t], recv_sem=rsem.at[t],
                device_id=(dp, d), device_id_type=MESH).start()
        for q in range(2):
            part = pl.ds(32 * q, 32)
            each(1, n_ax, one)
        pltpu.make_async_copy(send.at[t, me], recv.at[t, me], lsem.at[t]).start()

    last = 2 * GRIGHT + 1

    def lanes(n):
        return slice(128 * n, 128 * (n + 1))

    def last_copy(n):
        return pltpu.make_async_copy(
            send.at[last, me, :, lanes(n)], recv.at[last, me, :, lanes(n)], lsem.at[last + n])

    def start_last(n):
        def one(o):
            d = peer(o)
            pltpu.make_async_remote_copy(
                src_ref=send.at[last, d, :, lanes(n)], dst_ref=recv.at[last, me, :, lanes(n)],
                send_sem=ssem.at[last + n], recv_sem=rsem.at[last + n],
                device_id=(dp, d), device_id_type=MESH).start()
        each(1, n_ax, one)
        last_copy(n).start()

    def wait_last(n):
        last_copy(n).wait()
        part = recv.at[last, pl.ds(0, n_ax - 1), :, lanes(n)]
        pltpu.make_async_copy(part, part, rsem.at[last + n]).wait()

    def wait_last_sent(n):
        part = send.at[last, pl.ds(0, n_ax - 1), :, lanes(n)]
        pltpu.make_async_copy(part, part, ssem.at[last + n]).wait()

    def wait_recv(t):
        pltpu.make_async_copy(send.at[t, me], recv.at[t, me], lsem.at[t]).wait()
        part = recv.at[t, pl.ds(0, n_ax - 1)]
        pltpu.make_async_copy(part, part, rsem.at[t]).wait()

    def wait_send(t):
        part = send.at[t, pl.ds(0, n_ax - 1)]
        pltpu.make_async_copy(part, part, ssem.at[t]).wait()

    def bytes_of(ref, sem):
        pltpu.make_async_copy(ref, ref, sem).wait()

    def push(src, dst, k, dp_index, ax_index):
        pltpu.make_async_remote_copy(
            src_ref=src, dst_ref=dst, send_sem=asend.at[k], recv_sem=arecv.at[k],
            device_id=(dp_index, ax_index), device_id_type=MESH).start()

    def rows8(n):
        return pl.ds(pl.multiple_of(8 * n, 8), 8)

    def rows32(n):
        return pl.ds(pl.multiple_of(32 * n, 32), 32)

    right_blocks = pl.ds(4, 2)
    others = pl.ds(0, n_ax - 1)

    def right_start():
        def one(o):
            d = peer(o)
            push(dw.at[right_blocks, rows8(d)], r1.at[me], 0, dp, d)
        for o in far_first:
            one(o)
        r1[me] = dw[4:6, rows8(me)]

    def right_dp():
        bytes_of(r1.at[others], arecv.at[0])
        total = jnp.sum(r1[...], axis=0)
        s1[...] = total
        r2[dp] = total
        each(1, n_dp, lambda o: push(s1, r2.at[dp], 1, dp_peer(o), me))

    def right_back():
        bytes_of(r2.at[pl.ds(0, n_dp - 1)], arecv.at[1])
        s2[...] = jnp.sum(r2[...], axis=0) * factor
        target = fin.at[right_blocks, rows8(me)]
        pltpu.make_async_copy(s2, target, fsem.at[0]).start()
        for o in far_first:
            push(s2, target, 2, dp, peer(o))

    my_x, my_yl = dp % 4, dp // 4

    def x_peer(o):
        return my_yl * 4 + (my_x + o) % 4

    def x_start(p):
        def one(o):
            push(dw.at[pl.ds(2 * p, 2), rows32((my_x + o) % 4)], x1.at[p, my_x], 3 + p, x_peer(o), me)
        each(1, 4, one)
        x1[p, my_x] = dw[2 * p:2 * p + 2, rows32(my_x)]

    def left_axial():
        for p in range(2):
            bytes_of(x1.at[p, pl.ds(0, 3)], arecv.at[3 + p])
            xs[2 * p:2 * p + 2] = jnp.sum(x1[p], axis=0)

        def one(o):
            d = peer(o)
            push(xs.at[d // 4, rows8(d % 4)], a1.at[me], 5, dp, d)
        each(1, n_ax, one)
        a1[me] = xs[me // 4, rows8(me % 4)]

    def left_y():
        bytes_of(a1.at[others], arecv.at[5])
        total = jnp.sum(a1[...], axis=0)
        s3[...] = total
        a2[my_yl] = total
        push(s3, a2.at[my_yl], 6, (dp + 4) % 8, me)

    def left_back():
        bytes_of(a2.at[0], arecv.at[6])
        total = (a2[0] + a2[1]) * factor
        s4[...] = total
        xg[me // 4, rows8(me % 4)] = total
        each(1, n_ax, lambda o: push(s4, xg.at[me // 4, rows8(me % 4)], 7, dp, peer(o)))

    def left_x():
        bytes_of(a1.at[others], arecv.at[7])
        target = fin.at[pl.ds(0, 4), rows32(my_x)]
        pltpu.make_async_copy(xg, target, fsem.at[1]).start()
        each(1, 4, lambda o: push(xg, target, 8, x_peer(o), me))

    def reduce_end():
        for sem in (asend, arecv):
            bytes_of(fin.at[right_blocks, pl.ds(0, 8 * (n_ax - 1))], sem.at[2])
            bytes_of(fin.at[pl.ds(0, 4), pl.ds(0, 96)], sem.at[8])
        bytes_of(r1.at[others], asend.at[0])
        bytes_of(r2.at[pl.ds(0, n_dp - 1)], asend.at[1])
        for p in range(2):
            bytes_of(x1.at[p, pl.ds(0, 3)], asend.at[3 + p])
        bytes_of(a1.at[others], asend.at[5])
        bytes_of(a2.at[0], asend.at[6])
        bytes_of(a1.at[others], asend.at[7])
        pltpu.make_async_copy(s2, fin.at[right_blocks, rows8(me)], fsem.at[0]).wait()
        pltpu.make_async_copy(xg, fin.at[pl.ds(0, 4), rows32(my_x)], fsem.at[1]).wait()

    def strided(i):
        return pl.ds(i, 128, stride=8)

    def put(k, values):
        tbuf2[0, strided(k), :] = values[:, :128]
        tbuf2[1, strided(k), :] = values[:, 128:]

    def take(k):
        return jnp.concatenate([tbuf[0, strided(k), :], tbuf[1, strided(k), :]], axis=1)

    def flush(t):
        for n in range(2):
            send[t, :, :, 128 * n:128 * (n + 1)] = tbuf2[n].astype(BF16).reshape(16, 64, 128)

    def unpack(t):
        for n in range(2):
            tbuf[n] = recv[t, :, :, 128 * n:128 * (n + 1)].astype(F32).reshape(1024, 128)

    def load_pair(t, cp):
        both = recv[t, :, pl.ds(pl.multiple_of(16 * cp, 16), 16), :].astype(F32).reshape(16, 2, 8, 256)
        return both[:, 0], both[:, 1]

    def store_pair(t, cp, even, odd):
        both = jnp.concatenate([even, odd], axis=1).astype(BF16)
        send[t, :, pl.ds(pl.multiple_of(16 * cp, 16), 16), :] = both

    fetch("w_in")
    w_t[...] = w_in[...].astype(F32).T.astype(BF16)
    fetch("gain_in")
    gin[...] = jnp.broadcast_to(jnp.broadcast_to(gain_in[...], (128, 128)).T[:, :1], (128, 256))

    def norm_in(i):
        unit, inv = stats(pair[i].astype(F32).T)
        unit_in[i] = unit
        inv_in[i] = inv
        normed[i] = (unit * gin[...]).astype(BF16)

    def gated(i, k, lo, gate_ref, q_ref):
        projected = dot(w_t[lo:lo + 256], normed[i])
        gate = sigmoid(projected[128:])
        value = projected[:128] * gate
        gate_ref[i] = gate
        q_ref[i] = value * (1.0 - gate)
        put(k, value)

    def first_left(k):
        norm_in(k)
        gated(k, k, 0, gate_a, q_a)

    def first_right(k):
        gated(k, k, 256, gate_b, q_b)

    def second_right(k):
        norm_in(8 + k)
        gated(8 + k, k, 256, gate_b, q_b)

    def second_left(k):
        gated(8 + k, k, 0, gate_a, q_a)

    fetch("pair0")
    each(0, 8, first_left)
    flush(2 * LEFT)
    pl.semaphore_wait(barrier, n_ax - 1 + n_dp - 1)
    start(2 * LEFT)
    each(0, 8, first_right)
    flush(2 * RIGHT)
    start(2 * RIGHT)
    fetch("pair1")
    each(0, 8, second_right)
    flush(2 * RIGHT + 1)
    start(2 * RIGHT + 1)
    each(0, 8, second_left)
    flush(2 * LEFT + 1)
    start(2 * LEFT + 1)

    fetch("w_out")
    fetch("gain_x")
    fetch("cot")
    wo_t[...] = w_out[...].astype(F32).T.astype(BF16)
    gx[...] = jnp.broadcast_to(jnp.broadcast_to(gain_x[...], (128, 128)).T[:, :1], (128, 256))

    def gate_row(i):
        gate = sigmoid(dot(w_t[512:640], normed[i]))
        upstream = cot[i].astype(F32).T
        lift = upstream * gate
        gate_o[i] = gate
        c_g[i] = lift * (1.0 - gate)
        lift = lift.astype(BF16)
        glift[i] = lift
        s_x[i] = dot(w_out[...], lift) * gx[...]
    each(0, 16, gate_row)
    dw[...] = jnp.zeros_like(dw)

    wait_recv(2 * LEFT)
    wait_recv(2 * RIGHT)
    wait_recv(2 * RIGHT + 1)
    for h in range(2):
        if h == 1:
            wait_recv(2 * LEFT + 1)

        def product_pair(cp):
            lefts = load_pair(2 * LEFT + h, cp)
            if h == 0:
                right0, right1 = load_pair(2 * RIGHT, cp), load_pair(2 * RIGHT + 1, cp)
            prods = []
            for e in range(2):
                left = lefts[e].reshape(128, 256).astype(BF16)
                lc[2 * cp + e, 128 * h:128 * (h + 1)] = left
                if h == 0:
                    right = jnp.concatenate([right0[e], right1[e]], axis=1).reshape(256, 256).astype(BF16)
                    rc[2 * cp + e] = right
                else:
                    right = rc[2 * cp + e]
                prods.append(dot_nt(left, right).reshape(16, 8, 256))
            store_pair(2 * PROD + h, cp, prods[0], prods[1])
        each(0, 4, product_pair)
        start(2 * PROD + h)

    for h in range(2):
        wait_recv(2 * PROD + h)
        unpack(2 * PROD + h)

        def norm_row(k):
            i = 8 * h + k
            unit, inv = stats(take(k))
            xnorm[i] = (unit * gx[...]).astype(BF16)
            scaled = s_x[i]
            mean_one = jnp.mean(scaled, axis=0, keepdims=True)
            mean_two = jnp.mean(scaled * unit, axis=0, keepdims=True)
            put(k, (scaled - mean_one - unit * mean_two) * inv)
        each(0, 8, norm_row)
        flush(2 * GPROD + h)
        start(2 * GPROD + h)

    def lift_row(i):
        flat = xnorm[i]
        lifted = dot(wo_t[...], flat)
        upd[i] = (gate_o[i] * lifted).T.astype(BF16)
        ggate = (lifted * c_g[i]).astype(BF16)
        dw[0] += dot_nt(flat, glift[i])
        dw[1] += dot_nt(normed[i], ggate)
        gnorm[i] = dot(w_in[:, 512:640], ggate)

    for h in range(2):
        wait_recv(2 * GPROD + h)

        def gleft_pair(cp):
            grads = load_pair(2 * GPROD + h, cp)
            outs = []
            for e in range(2):
                grad = grads[e].reshape(128, 256).astype(BF16)
                gc[2 * cp + e, 128 * h:128 * (h + 1)] = grad
                outs.append(dot(grad, rc[2 * cp + e]).reshape(16, 8, 256))
            store_pair(2 * GLEFT + h, cp, outs[0], outs[1])
        each(0, 4, gleft_pair)
        start(2 * GLEFT + h)
        each(8 * h, 8 * h + 8, lift_row)

    x_start(0)

    def gright_pair(cp):
        outs = [dot_tn(gc[2 * cp + e], lc[2 * cp + e]).reshape(16, 2, 8, 256) for e in range(2)]
        for h in range(2):
            store_pair(2 * GRIGHT + h, cp, outs[0][:, h], outs[1][:, h])
    each(0, 4, gright_pair)
    start(2 * GRIGHT)
    start_last(0)
    start_last(1)
    put_out("upd")

    def back_a(h):
        def grad_row(k):
            i = 8 * h + k
            grad = take(k)
            both = jnp.concatenate([grad * gate_a[i], grad * q_a[i]], axis=0).astype(BF16)
            local = dot_nt(normed[i], both)
            dw[2] += local[:, :128]
            dw[3] += local[:, 128:]
            gnorm[i] += dot(w_in[:, 0:256], both)
        wait_recv(2 * GLEFT + h)
        unpack(2 * GLEFT + h)
        each(0, 8, grad_row)

    def back_b(h):
        total = jnp.concatenate([dw[4], dw[5]], axis=1)
        if h == 0:
            wait_recv(2 * GRIGHT)
        for n in range(2):
            if h == 1:
                wait_last(n)
            tbuf[n] = recv[2 * GRIGHT + h, :, :, lanes(n)].astype(F32).reshape(1024, 128)
            for k in range(0, 8, 2):
                sides = []
                for e in (k, k + 1):
                    i = 8 * h + e
                    grad = tbuf[n, strided(e), :]
                    both = jnp.concatenate(
                        [grad * gate_b[i, :, lanes(n)], grad * q_b[i, :, lanes(n)]], axis=0).astype(BF16)
                    gproj[e, :, lanes(n)] = both
                    sides.append((normed[i, :, lanes(n)], both))
                total += dot_nt(
                    jnp.concatenate([sides[0][0], sides[1][0]], axis=1),
                    jnp.concatenate([sides[0][1], sides[1][1]], axis=1))
        dw[4] = total[:, :128]
        dw[5] = total[:, 128:]

    def out_rows(h):
        def out_row(k):
            i = 8 * h + k
            unit = unit_in[i]
            scaled = (gnorm[i] + dot(w_in[:, 256:512], gproj[k])) * gin[...]
            mean_one = jnp.mean(scaled, axis=0, keepdims=True)
            mean_two = jnp.mean(scaled * unit, axis=0, keepdims=True)
            gpair[i] = ((scaled - mean_one - unit * mean_two) * inv_in[i]).T.astype(BF16)
        each(0, 8, out_row)
        put_out("gpair%d" % h)

    back_a(0)
    back_a(1)
    x_start(1)
    back_b(0)
    left_axial()
    out_rows(0)
    back_b(1)
    right_start()
    left_y()
    out_rows(1)
    left_back()
    right_dp()
    left_x()
    right_back()
    for t in range(11):
        wait_send(t)
    for n in range(2):
        wait_last_sent(n)
    for name in put_names:
        out_copy(name).wait()
    reduce_end()


def hand_on(
    upd_h, gpair_h, fin_h, w_in_h, w_out_h, gain_in_h, gain_x_h,
    upd_o, gpair_o, gw_in_o, gw_out_o, ggi_o, ggx_o,
    upd, gpair, gw_in, gw_out, ggi, ggx, fin, w_in, w_out, gain_in, gain_x, isem, osem,
):
    def moves(pairs, sems, first):
        return [pltpu.make_async_copy(a, b, sems.at[first + n]) for n, (a, b) in enumerate(pairs)]

    small_in = moves(((fin_h, fin), (w_in_h, w_in), (w_out_h, w_out), (gain_in_h, gain_in),
                      (gain_x_h, gain_x)), isem, 0)
    halves = pl.ds(0, 8), pl.ds(8, 8)
    big_in = moves([(a.at[h], b.at[h]) for a, b in ((upd_h, upd), (gpair_h, gpair)) for h in halves], isem, 5)
    big_out = moves([(a.at[h], b.at[h]) for a, b in ((upd, upd_o), (gpair, gpair_o)) for h in halves], osem, 0)
    small_out = moves(((gw_in, gw_in_o), (gw_out, gw_out_o), (ggi, ggi_o), (ggx, ggx_o)), osem, 4)
    for copy in small_in + big_in:
        copy.start()
    for copy in small_in:
        copy.wait()
    gw_out[...] = fin[0]
    gw_in[:, 512:640] = fin[1]
    for n in range(4):
        gw_in[:, 128 * n:128 * (n + 1)] = fin[2 + n]
    small_out[0].start()
    small_out[1].start()
    for n in range(4):
        big_in[n].wait()
        big_out[n].start()
    row_x = jnp.sum(gw_out[...] * w_out[...].astype(F32), axis=1, keepdims=True)
    ggx[...] = jnp.broadcast_to(row_x, (128, 128)).T[:1] / gain_x[...]
    row_in = jnp.sum(gw_in[...] * w_in[...].astype(F32), axis=1, keepdims=True)
    ggi[...] = jnp.broadcast_to(row_in, (128, 128)).T[:1] / gain_in[...]
    small_out[2].start()
    small_out[3].start()
    for copy in big_out + small_out:
        copy.wait()


def local(n_dp, n_ax, pair, cotangent, in_weight, out_weight, gain_in, gain_x):
    rows, width, chan = pair.shape[1:]
    factor = 1.0 / (n_dp * width * width) ** 0.5
    anywhere = pl.BlockSpec(memory_space=pl.ANY)
    cells = (rows, chan, width)
    args = (pair[0], cotangent[0], in_weight, out_weight, gain_in[None], gain_x[None])
    out_shape = (
        jax.ShapeDtypeStruct((rows, width, chan), BF16),
        jax.ShapeDtypeStruct((rows, width, chan), BF16),
        jax.ShapeDtypeStruct((128, 640), F32),
        jax.ShapeDtypeStruct((128, 128), F32),
        jax.ShapeDtypeStruct((1, 128), F32),
        jax.ShapeDtypeStruct((1, 128), F32),
    )
    sums_shape = jax.ShapeDtypeStruct((6, 128, 128), F32)
    upd, gpair, sums = pl.pallas_call(
        functools.partial(kernel, n_dp, n_ax, factor),
        name="triangle",
        out_shape=out_shape[:2] + (sums_shape,),
        in_specs=[anywhere] * 6,
        out_specs=(anywhere,) * 3,
        scratch_shapes=[pltpu.VMEM(v.shape, v.dtype) for v in args + out_shape[:2]] + [
            pltpu.SemaphoreType.DMA((7,)),
            pltpu.SemaphoreType.DMA((3,)),
            pltpu.SemaphoreType.DMA((2,)),
            pltpu.VMEM((8, 256, 256), BF16),
            pltpu.VMEM((12, 16, 64, 256), BF16),
            pltpu.VMEM((12, 16, 64, 256), BF16),
            pltpu.VMEM((2, 1024, 128), F32),
            pltpu.VMEM((2, 1024, 128), F32),
            pltpu.VMEM((8, 256, 256), BF16),
            pltpu.VMEM((8, 256, 256), BF16),
            pltpu.VMEM((8, 256, 256), BF16),
            pltpu.VMEM(cells, BF16),
            pltpu.VMEM(cells, F32),
            pltpu.VMEM((rows, 1, width), F32),
            pltpu.VMEM(cells, F32),
            pltpu.VMEM(cells, F32),
            pltpu.VMEM(cells, F32),
            pltpu.VMEM(cells, F32),
            pltpu.VMEM(cells, F32),
            pltpu.VMEM(cells, F32),
            pltpu.VMEM(cells, F32),
            pltpu.VMEM(cells, BF16),
            pltpu.VMEM(cells, BF16),
            pltpu.VMEM(cells, F32),
            pltpu.VMEM((640, 128), BF16),
            pltpu.VMEM((128, 128), BF16),
            pltpu.VMEM((128, 256), F32),
            pltpu.VMEM((128, 256), F32),
            pltpu.VMEM((6, 128, 128), F32),
            pltpu.VMEM((16, 2, 8, 128), F32),
            pltpu.VMEM((8, 2, 8, 128), F32),
            pltpu.VMEM((2, 8, 128), F32),
            pltpu.VMEM((2, 8, 128), F32),
            pltpu.VMEM((2, 4, 2, 32, 128), F32),
            pltpu.VMEM((4, 32, 128), F32),
            pltpu.VMEM((16, 8, 128), F32),
            pltpu.VMEM((2, 8, 128), F32),
            pltpu.VMEM((8, 128), F32),
            pltpu.VMEM((8, 128), F32),
            pltpu.VMEM((4, 32, 128), F32),
            pltpu.SemaphoreType.DMA((13,)),
            pltpu.SemaphoreType.DMA((13,)),
            pltpu.SemaphoreType.DMA((13,)),
            pltpu.SemaphoreType.DMA((9,)),
            pltpu.SemaphoreType.DMA((9,)),
        ],
        compiler_params=pltpu.CompilerParams(
            collective_id=0, has_side_effects=True, vmem_limit_bytes=60 * 2**20),
        cost_estimate=pl.CostEstimate(
            flops=3_300_000_000, bytes_accessed=5_000_000, transcendentals=1_600_000),
    )(*args)
    upd, gpair, gw_in, gw_out, ggi, ggx = pl.pallas_call(
        hand_on,
        name="hand_on",
        out_shape=out_shape,
        in_specs=[anywhere] * 7,
        out_specs=(anywhere,) * 6,
        scratch_shapes=[pltpu.VMEM(v.shape, v.dtype) for v in out_shape] + [
            pltpu.VMEM((6, 128, 128), F32)] + [pltpu.VMEM(v.shape, v.dtype) for v in args[2:]] + [
            pltpu.SemaphoreType.DMA((9,)),
            pltpu.SemaphoreType.DMA((8,)),
        ],
        compiler_params=pltpu.CompilerParams(vmem_limit_bytes=60 * 2**20),
    )(upd, gpair, sums, *args[2:])
    return upd[None], gpair[None], gw_in, gw_out, ggi[0], ggx[0]


def solution(mesh):
    cells = P("dp", "axial", None, None)
    n_dp, n_ax = mesh.shape["dp"], mesh.shape["axial"]
    return jax.shard_map(
        functools.partial(local, n_dp, n_ax), mesh=mesh,
        in_specs=(cells, cells, P(), P(), P(), P()),
        out_specs=(cells, cells, P(), P(), P(), P()), check_vma=False)
```
